256 devices in a mesh: vocab: 32 (over y, z), seq: 8 (over x, core).
Axes of the slice: x: 4, y: 4, z: 8, core: 2. Of those that a mesh axis runs over, the one named last changes fastest.
Arguments:
- old_table: bfloat16 [65536, 8192], P('vocab', 'seq'), may hold values from -1000 to 1000
- pieces: int32 [4096, 8], P('vocab'), may hold values from 0 to 65535, as said below
- lengths: int32 [4096], P('vocab'), may hold values from 1 to 8, as said below
- pos_gain: float32 [8], replicated, may hold values from 0.3 to 1.5
- hyp_gain: float32 [8192], P('seq'), may hold values from 0.5 to 1.5
- w_in: bfloat16 [8192, 8192], P('seq', 'vocab'), may hold values from -0.0625 to 0.0625
- w_out: bfloat16 [8192, 8192], P('seq', 'vocab'), may hold values from -0.0029296875 to 0.0029296875
- hidden: bfloat16 [32768, 8192], P('vocab', 'seq'), may hold values from -100 to 100
- token_ids: int32 [32768], P('seq'), may hold values from 0 to 4095
- targets: int32 [32768], P('vocab'), may hold values from 0 to 4095
Outputs:
- embedded: bfloat16 [32768, 8192], P('seq', 'vocab')
- loss: float32 [32768], P(('vocab', 'seq'))
The draws below stay inside these ranges and needn't reach their ends.
Inputs may be any that keep to these rules, and one draw needn't show every extreme that they name: New token j has lengths[j] pieces, the first entries of its row of pieces; every aligned group of 128 new tokens has one token with 8 pieces. Only the first lengths[j] entries of row j count, the others are arbitrary ids; the counted pieces of one aligned group of 128 new tokens lie at most 32 in one aligned block of 2048 old ids, and exactly 32 in some block.
All inputs are finite; a program needn't handle non-finite values.
Results may differ from the reference program's by a relative error of at most 0.0049.
Values may be sent and summed in bfloat16 or wider, within the bound.
No kernel may reach another device: no remote copies, remote signals or barrier semaphores. Data moves between devices by JAX's collectives and lax.ppermute only.
A program may use at most 128 MiB of HBM per device.

```python
import math
import jax
import jax.numpy as jnp
from jax import lax

D = 8192
OLDV = 65536
P_SIZE = 8
VOC_DEV = 128
V = 4096
TOKENS = 32768
N_VOCAB = 32


def decomposition(key):
    shard_rows = OLDV // N_VOCAB
    slot_total = VOC_DEV * P_SIZE
    capacity = VOC_DEV * P_SIZE // N_VOCAB

    def draw_block(block_index):
        block_key = jax.random.fold_in(key, block_index)
        subkeys = jax.random.split(block_key, 8)
        factor_one = jax.random.randint(subkeys[0], (N_VOCAB,), 0, capacity + 1)
        factor_two = jax.random.randint(subkeys[1], (N_VOCAB,), 0, capacity + 1)
        counts = jnp.minimum(capacity // 8 + factor_one * factor_two // capacity, capacity)
        hot_block = jax.random.randint(subkeys[2], (), 0, N_VOCAB)
        counts = jnp.where(jnp.arange(N_VOCAB, dtype=jnp.int32) == hot_block, capacity, counts)
        live_total = jnp.sum(counts)
        extra_total = VOC_DEV * (P_SIZE - 1)
        extra_order = jax.random.permutation(subkeys[3], extra_total).astype(jnp.int32)
        full_token = jax.random.randint(subkeys[4], (), 0, VOC_DEV)
        extra_token = jnp.arange(extra_total, dtype=jnp.int32) // (P_SIZE - 1)
        priority = jnp.where(extra_token == full_token, extra_order - extra_total, extra_order)
        extra_rank = jnp.argsort(jnp.argsort(priority, stable=True), stable=True)
        chosen_extra = (extra_rank < live_total - VOC_DEV).astype(jnp.int32)
        piece_lengths = 1 + jnp.sum(chosen_extra.reshape(VOC_DEV, P_SIZE - 1), axis=1)
        live_slots = (jnp.arange(P_SIZE, dtype=jnp.int32)[None, :] < piece_lengths[:, None]).reshape(-1)
        cumulative = jnp.cumsum(counts)
        position = jnp.arange(slot_total, dtype=jnp.int32)
        owner_of_rank = jnp.sum((position[:, None] >= cumulative[None, :]).astype(jnp.int32), axis=1)
        live_order = jax.random.permutation(subkeys[5], slot_total).astype(jnp.int32)
        live_priority = jnp.where(live_slots, live_order, live_order + slot_total)
        live_rank = jnp.argsort(jnp.argsort(live_priority, stable=True), stable=True)
        dead_owner = jax.random.randint(subkeys[6], (slot_total,), 0, N_VOCAB)
        owner_block = jnp.where(live_slots, jnp.take(owner_of_rank, live_rank), dead_owner)
        local_row = jax.random.randint(subkeys[7], (slot_total,), 0, shard_rows)
        block_pieces = (owner_block * shard_rows + local_row).reshape(VOC_DEV, P_SIZE)
        return (block_pieces.astype(jnp.int32), piece_lengths.astype(jnp.int32))
    all_pieces, all_lengths = jax.vmap(draw_block)(jnp.arange(N_VOCAB, dtype=jnp.int32))
    return (all_pieces.reshape(V, P_SIZE), all_lengths.reshape(V))


def draw_pieces(key, part):
    return decomposition(key)[0]


def draw_lengths(key, part):
    return decomposition(key)[1]


def draw_old_table(key, part):
    key = jax.random.fold_in(key, 23)
    subkeys = jax.random.split(key, 2)
    column = jnp.arange(D, dtype=jnp.float32)[None, :] / (D - 1)
    base = jnp.clip(jax.random.normal(subkeys[0], (OLDV, D), jnp.float32), -4.0, 4.0)
    row_scale = jnp.exp(jax.random.uniform(subkeys[1], (OLDV, 1), jnp.float32, 0.0, math.log(10.0)))
    values = base * row_scale * jnp.exp(math.log(10.0) * column)
    return values.astype(jnp.bfloat16)


def draw_hidden(key, part):
    key = jax.random.fold_in(key, 11)
    subkeys = jax.random.split(key, 1)
    return jnp.clip(jax.random.normal(subkeys[0], (TOKENS, D), jnp.float32), -6.0, 6.0).astype(jnp.bfloat16)


def touch_ends(entries, rng, least, high):
    extent = entries.shape
    index_at = [jax.random.randint(jax.random.fold_in(rng, axis), (), 0, extent[axis]) for axis in range(len(extent))]
    entries = entries.at[tuple(index_at)].set(least)
    longest = extent.index(max(extent))
    index_at[longest] = (index_at[longest] + 1) % extent[longest]
    return entries.at[tuple(index_at)].set(high)


def block_levels(stream_key, extent, cuts, least, largest):
    level, own = 1.0, jax.random.fold_in(stream_key, 6)
    for dim, blocks in cuts:
        draws = jnp.exp(jax.random.uniform(jax.random.fold_in(own, dim), (blocks,), jnp.float32, least / len(cuts), largest / len(cuts)))
        level = level * jnp.repeat(draws, extent[dim] // blocks).reshape([-1 if axis == dim else 1 for axis in range(len(extent))])
    return level


def noise(key, dims, scale, reach, cuts=(), kind=jnp.bfloat16):
    array = jax.random.normal(key, dims, jnp.float32) * scale
    if len(cuts) > 0:
        array = block_levels(key, dims, cuts, -0.22, 0.18) * array
    return jnp.clip(array, min=-reach, max=reach).astype(kind)


def setup_inputs(seed: int = 0) -> dict:
    key_of = jax.random.split(jax.random.key(seed), 11)
    old_table = draw_old_table(jax.random.fold_in(key_of[10], 71), 0)
    pieces = draw_pieces(jax.random.fold_in(key_of[10], 71), 0)
    lengths = draw_lengths(jax.random.fold_in(key_of[10], 71), 0)
    pos_gain = jnp.clip(jnp.exp(jax.random.uniform(key_of[3], (P_SIZE,), jnp.float32, math.log(0.3), math.log(1.5))), 0.3, 1.5)
    hyp_gain = jnp.clip(1.0 + 0.1 * jax.random.normal(key_of[4], (D,), jnp.float32), 0.5, 1.5)
    w_in = noise(key_of[5], (D, D), D ** -0.5, 0.0625, ((0, 8), (1, 32)))
    w_out = noise(key_of[6], (D, D), (D * D // 16) ** -0.5, 0.0029296875, ((0, 8), (1, 32)))
    hidden = draw_hidden(jax.random.fold_in(key_of[10], 71), 0)
    token_ids = touch_ends(jax.random.randint(key_of[8], (TOKENS,), 0, V), jax.random.fold_in(key_of[8], 1), 0, V - 1).astype(jnp.int32)
    targets = touch_ends(jax.random.randint(key_of[9], (TOKENS,), 0, V), jax.random.fold_in(key_of[9], 1), 0, V - 1).astype(jnp.int32)
    return dict(old_table=old_table, pieces=pieces, lengths=lengths, pos_gain=pos_gain, hyp_gain=hyp_gain, w_in=w_in, w_out=w_out, hidden=hidden, token_ids=token_ids, targets=targets)


epsilon = 1e-05

def reference(old_table, pieces, lengths, pos_gain, hyp_gain, w_in, w_out, hidden, token_ids, targets):
    slot_index = jnp.arange(P_SIZE, dtype=jnp.int32)
    live_slots = slot_index[None, :] < lengths[:, None]
    weights = jnp.where(live_slots, pos_gain[None, :], jnp.zeros_like(pos_gain)[None, :])
    gathered = jnp.take(old_table, pieces, axis=0).astype(jnp.float32)
    pooled = lax.optimization_barrier(jnp.sum(gathered * weights[:, :, None], axis=1))
    mean_square = lax.optimization_barrier(jnp.sum(pooled * pooled, axis=1, keepdims=True)) / D
    normed = (pooled * lax.rsqrt(mean_square + epsilon) * hyp_gain[None, :]).astype(jnp.bfloat16)
    input_rows = jnp.dot(normed, w_in, preferred_element_type=jnp.float32).astype(jnp.bfloat16)
    output_rows = jnp.dot(normed, w_out, preferred_element_type=jnp.float32).astype(jnp.bfloat16)
    embedded = jnp.take(input_rows, token_ids, axis=0)
    logits = jnp.dot(hidden, output_rows.T, preferred_element_type=jnp.float32)
    row_max = lax.optimization_barrier(jnp.max(logits, axis=1))
    spread = lax.optimization_barrier(jnp.sum(jnp.exp(logits - row_max[:, None]), axis=1))
    target_logit = jnp.take_along_axis(logits, targets[:, None], axis=1)[:, 0]
    loss = row_max + jnp.log(spread) - target_logit
    return (embedded, loss)
```

```python
import jax
import jax.numpy as jnp
from jax import lax
from jax.experimental import pallas as pl
from jax.experimental.pallas import tpu as pltpu
from jax.sharding import Mesh
from jax.sharding import PartitionSpec as P

EPSILON = 1e-05
NY, NZ, NX, NC = 4, 8, 4, 2
BLOCKS = NY * NZ
PARTS = NX * NC
D = 8192
VOC = 128
PIECES = 8
SHARD = 2048
CAP = 32
FEAT = D // PARTS
WIDE = D // NZ
EXTRA = 128
TOK = 1024
ROWS_A = 80
MIB = 1 << 20

VMEM = pl.BlockSpec(memory_space=pltpu.VMEM)
SMEM = pl.BlockSpec(memory_space=pltpu.SMEM)
ANY = pl.BlockSpec(memory_space=pl.ANY)


def dot(left, right):
    return jnp.dot(left, right, preferred_element_type=jnp.float32)


def dot_dims(left, right, left_dim, right_dim):
    return lax.dot_general(
        left, right, (((left_dim,), (right_dim,)), ((), ())), preferred_element_type=jnp.float32
    )


def call(kernel, out_shape, in_specs, scratch=(), limit=32 * MIB):
    many = isinstance(out_shape, (tuple, list))
    return pl.pallas_call(
        kernel,
        out_shape=out_shape,
        in_specs=in_specs,
        out_specs=[VMEM] * len(out_shape) if many else VMEM,
        scratch_shapes=list(scratch),
        compiler_params=pltpu.CompilerParams(vmem_limit_bytes=limit),
    )


def shape(dims, kind):
    return jax.ShapeDtypeStruct(dims, kind)


def plan_kernel(pieces_ref, lengths_ref, request_ref, where_ref):
    row = lax.broadcasted_iota(jnp.int32, (VOC, VOC), 0)
    col = lax.broadcasted_iota(jnp.int32, (VOC, VOC), 1)
    earlier = (row > col).astype(jnp.float32).astype(jnp.bfloat16)
    lane = lax.broadcasted_iota(jnp.int32, (VOC, BLOCKS), 1)
    lane8 = lax.broadcasted_iota(jnp.int32, (VOC, PIECES), 1)
    lengths = lengths_ref[...]
    base = jnp.zeros((1, BLOCKS), jnp.float32)
    high_sum = jnp.zeros((BLOCKS, CAP), jnp.float32)
    low_sum = jnp.zeros((BLOCKS, CAP), jnp.float32)
    where = jnp.full((VOC, PIECES), -1, jnp.int32)
    for k in range(PIECES):
        piece = pieces_ref[:, k : k + 1]
        live = lengths > k
        block = jnp.where(live, piece >> 11, BLOCKS)
        local = piece & (SHARD - 1)
        onehot = (block == lane).astype(jnp.float32)
        onehot16 = onehot.astype(jnp.bfloat16)
        before = dot(earlier, onehot16) + base
        rank = jnp.sum(before * onehot, axis=1, keepdims=True).astype(jnp.int32)
        base = base + jnp.sum(onehot, axis=0, keepdims=True)
        at_rank = rank == lane
        high = jnp.where(at_rank, (local >> 6).astype(jnp.float32), 0.0).astype(jnp.bfloat16)
        low = jnp.where(at_rank, (local & 63).astype(jnp.float32), 0.0).astype(jnp.bfloat16)
        high_sum = high_sum + dot_dims(onehot16, high, 0, 0)
        low_sum = low_sum + dot_dims(onehot16, low, 0, 0)
        place = jnp.where(live, block * CAP + rank, -1)
        where = jnp.where(lane8 == k, place, where)
    request_ref[...] = high_sum.astype(jnp.int32) * 64 + low_sum.astype(jnp.int32)
    where_ref[...] = where


def spread_kernel(gain_ref, where_ref, out_ref):
    lane = lax.broadcasted_iota(jnp.int32, (VOC, BLOCKS * CAP), 1)
    total = jnp.zeros((VOC, BLOCKS * CAP), jnp.float32)
    for k in range(PIECES):
        total = jnp.where(where_ref[:, k : k + 1] == lane, gain_ref[k], total)
    for term in range(3):
        part = total.astype(jnp.bfloat16)
        out_ref[term] = part
        total = total - part.astype(jnp.float32)


def pool_kernel(spread_ref, rows_ref, gain_ref, out_ref):
    rows = rows_ref[...]
    pooled = dot(spread_ref[2], rows) + dot(spread_ref[1], rows) + dot(spread_ref[0], rows)
    out_ref[...] = (pooled * gain_ref[...]).astype(jnp.bfloat16)


def split_two(value, lane):
    high = value.astype(jnp.bfloat16)
    low = (value - high.astype(jnp.float32)).astype(jnp.bfloat16)
    return jnp.where(
        lane == 0, high.astype(jnp.float32), jnp.where(lane == 1, low.astype(jnp.float32), 0.0)
    ).astype(jnp.bfloat16)


def project_kernel(
    extra, place_ref, weight_ref, scale_ref, b0, p1, m1, p2, m2, p3, m3, p4, m4, keep_ref, give_ref,
    rows_buf, result_buf,
):
    z, core = place_ref[0], place_ref[1]
    blocks = [(0, b0), (-1, p1), (1, m1), (-2, p2), (2, m2), (-3, p3), (3, m3)]
    for step, ref in blocks:
        at = lax.rem(z + (step + NZ), NZ)
        rows_buf[pl.ds(pl.multiple_of(at * VOC, VOC), VOC), :] = ref[...]
    at = lax.rem(z + 4, NZ)
    half = VOC // 2
    rows_buf[pl.ds(pl.multiple_of(at * VOC, half), half), :] = p4[...]
    rows_buf[pl.ds(pl.multiple_of(at * VOC + half, half), half), :] = m4[...]
    for q in range(NY):
        columns = slice(q * 256, (q + 1) * 256)
        result = dot(rows_buf[...], weight_ref[q])
        for i in range(PARTS):
            result_buf[i, :, columns] = result[i * VOC : (i + 1) * VOC]
    if extra:
        lane = lax.broadcasted_iota(jnp.int32, (VOC, EXTRA), 1)
        scale = scale_ref[...]
        for i in range(PARTS):
            wide = rows_buf[i * VOC : (i + 1) * VOC, :].astype(jnp.float32)
            square = jnp.sum(wide * wide * scale, axis=1, keepdims=True)
            result_buf[i, :, WIDE:] = split_two(square, lane).astype(jnp.float32)
    for i in range(NX):
        keep_ref[i] = result_buf[2 * i + core]
        give_ref[i] = result_buf[2 * i + 1 - core].astype(jnp.bfloat16)


def add_kernel(extra, keep_ref, got_ref, out_ref):
    lane = lax.broadcasted_iota(jnp.int32, (VOC, EXTRA), 1)
    for i in range(NX):
        total = keep_ref[i] + got_ref[i].astype(jnp.float32)
        out_ref[i, :, :WIDE] = total[:, :WIDE].astype(jnp.bfloat16)
        if extra:
            square = jnp.sum(total[:, WIDE:], axis=1, keepdims=True)
            out_ref[i, :, WIDE:] = split_two(square, lane)


def norm_kernel(parts_ref, out_ref, inverse_ref):
    total = parts_ref[0].astype(jnp.float32)
    for i in range(1, NX):
        total = total + parts_ref[i].astype(jnp.float32)
    square = jnp.sum(total[:, WIDE:], axis=1, keepdims=True)
    inverse = lax.rsqrt(square / D + EPSILON)
    out_ref[...] = (total[:, :WIDE] * inverse).astype(jnp.bfloat16)
    inverse_ref[...] = inverse


def scale_kernel(parts_ref, inverse_ref, out_ref):
    total = parts_ref[0].astype(jnp.float32)
    for i in range(1, NX):
        total = total + parts_ref[i].astype(jnp.float32)
    rows = (total * inverse_ref[...]).astype(jnp.bfloat16)
    for q in range(NY):
        out_ref[q] = rows[:, q * 256 : (q + 1) * 256]


def shift_by(value, axis, step):
    count = {"y": NY, "z": NZ, "x": NX, "c": NC}[axis]
    return lax.ppermute(value, axis, [(i, (i + step) % count) for i in range(count)])


def z_ring(rows, first):
    p1, m1 = shift_by(rows, "z", 1), shift_by(rows, "z", -1)
    p2, m2 = shift_by(p1, "z", 1), shift_by(m1, "z", -1)
    p3, m3 = shift_by(p2, "z", 1), shift_by(m2, "z", -1)
    p4, m4 = shift_by(p3[:first], "z", 1), shift_by(m3[first:], "z", -1)
    return [rows, p1, m1, p2, m2, p3, m3, p4, m4]


def y_ring(rows, first):
    p1, m1 = shift_by(rows, "y", 1), shift_by(rows, "y", -1)
    p2, m2 = shift_by(p1[:first], "y", 1), shift_by(m1[first:], "y", -1)
    return [rows, p1, m1, p2, m2]


def z_pieces(height, first):
    out = [(s, 0, height) for s in (0, -1, 1, -2, 2, -3, 3)]
    return out + [(4, 0, first), (4, first, height - first)]


def y_pieces(height, first):
    out = [(s, 0, height) for s in (0, -1, 1)]
    return out + [(2, 0, first), (2, first, height - first)]


def pieces_of_stack(parts):
    out, at = [], 0
    for shift, start, rows in parts:
        out.append((shift, at, start, rows))
        at += rows
    return out


def overlap(entries, low, high):
    out = []
    for shift, at, start, rows in entries:
        a, b = max(at, low), min(at + rows, high)
        if a < b:
            out.append((shift, a - low, start + a - at, b - a))
    return out


def accumulate(shifts, routes, arrays, place_ref, hidden_ref, total_ref, bufs):
    hidden_buf, rows_buf, hidden_sem, rows_sem = bufs
    y, z = place_ref[2], place_ref[0]
    waits = [[] for _ in shifts]
    for number, (index, from_row, rows, dy, dz, to_row) in enumerate(routes):
        slot = shifts.index(dz)
        at_y = lax.rem(y + (dy + NY), NY)
        start = pl.multiple_of(at_y * VOC + to_row, 16)
        copy = pltpu.make_async_copy(
            arrays[index].at[pl.ds(from_row, rows)],
            rows_buf.at[slot, pl.ds(start, rows)],
            rows_sem.at[number],
        )
        copy.start()
        waits[slot].append(copy)
    for slot, dz in enumerate(shifts):
        at = lax.rem(z + (dz + NZ), NZ)
        for q in range(NY):
            copy = pltpu.make_async_copy(
                hidden_ref.at[2 * q + at // 4, :, pl.ds(pl.multiple_of((at % 4) * 256, 256), 256)],
                hidden_buf.at[slot, :, pl.ds(q * 256, 256)],
                hidden_sem.at[slot, q],
            )
            copy.start()
            waits[slot].append(copy)
    tile = 256
    for slot in range(len(shifts)):
        for copy in waits[slot]:
            copy.wait()
        for i in range(TOK // tile):
            rows = pl.ds(i * tile, tile)
            product = dot_dims(hidden_buf[slot, rows, :], rows_buf[slot], 1, 1)
            total_ref[rows, :] = total_ref[rows, :] + product


def near_kernel(shifts, routes, count, place_ref, hidden_ref, *refs):
    arrays, total_ref = refs[:count], refs[count]
    total_ref[...] = jnp.zeros_like(total_ref)
    accumulate(shifts, routes, arrays, place_ref, hidden_ref, total_ref, refs[count + 1 :])


def far_kernel(shifts, routes, count, place_ref, target_ref, total_in, hidden_ref, *refs):
    arrays, out_ref, total_ref = refs[:count], refs[count], refs[count + 1]
    total_ref[...] = total_in[...]
    accumulate(shifts, routes, arrays, place_ref, hidden_ref, total_ref, refs[count + 2 :])
    part = place_ref[3]
    tile = 256
    column = lax.broadcasted_iota(jnp.int32, (tile, NY * VOC), 1)
    token_of = (column // VOC) * (NZ * VOC) + part * VOC + column % VOC
    lane = lax.broadcasted_iota(jnp.int32, (tile, 128), 1)
    for i in range(TOK // tile):
        rows = pl.ds(i * tile, tile)
        total = total_ref[rows, :]
        best = jnp.max(total, axis=1, keepdims=True)
        spread = jnp.sum(jnp.exp(total - best), axis=1, keepdims=True)
        hit = jnp.sum(jnp.where(token_of == target_ref[rows, :], total, 0.0), axis=1, keepdims=True)
        packed = jnp.where(lane == 0, best, jnp.where(lane == 1, spread, hit))
        turned = packed.T
        for j in range(tile // 128):
            out_ref[i * (tile // 128) + j] = turned[:8, j * 128 : (j + 1) * 128]


def merge_kernel(parts_ref, out_ref):
    best = parts_ref[0, 0:1, :]
    for i in range(1, PARTS):
        best = jnp.maximum(best, parts_ref[i, 0:1, :])
    spread = jnp.zeros_like(best)
    hit = jnp.zeros_like(best)
    for i in range(PARTS):
        spread = spread + parts_ref[i, 1:2, :] * jnp.exp(parts_ref[i, 0:1, :] - best)
        hit = hit + parts_ref[i, 2:3, :]
    out_ref[...] = best + jnp.log(spread) - hit


def add_core(keep, give, extra):
    got = shift_by(give, "c", 1)
    return call(
        lambda *refs: add_kernel(extra, *refs), shape(keep.shape, jnp.bfloat16), [VMEM, VMEM]
    )(keep, got)


def swap(value, axes):
    return lax.all_to_all(value, axes, split_axis=0, concat_axis=0, tiled=True)


def after(value, *others):
    return lax.optimization_barrier((value, *others))[0]


def on_device(
    old_table, pieces, lengths, pos_gain, hyp_gain, w_in, w_out, hidden, token_ids, targets
):
    y, z = lax.axis_index("y"), lax.axis_index("z")
    core = lax.axis_index("c")
    part = lax.axis_index(("x", "c"))
    place = jnp.stack([z, core, y, part]).astype(jnp.int32)
    gain_row = hyp_gain.reshape(1, FEAT)
    target_column = targets.reshape(TOK, 1)

    w_out_all = lax.all_gather(w_out, "y", axis=0)
    hidden_all = lax.all_gather(after(hidden, w_out), ("x", "c"), axis=0)

    requests, where = call(
        plan_kernel,
        [shape((BLOCKS, CAP), jnp.int32), shape((VOC, PIECES), jnp.int32)],
        [VMEM, VMEM],
    )(pieces, lengths.reshape(VOC, 1))
    wanted = swap(requests.reshape(BLOCKS, 1, CAP), ("y", "z"))
    found = old_table.at[wanted.reshape(-1)].get(mode="promise_in_bounds")
    fetched = swap(found.reshape(BLOCKS, CAP, FEAT), ("y", "z"))
    spread = call(
        spread_kernel, shape((3, VOC, BLOCKS * CAP), jnp.bfloat16), [SMEM, VMEM]
    )(pos_gain, where)
    in_ring = y_ring(after(w_in, found), FEAT // 2)
    w_in_all = [in_ring[0], in_ring[2], jnp.concatenate(in_ring[3:], axis=0), in_ring[1]]
    w_in_all = jnp.roll(jnp.stack(w_in_all), y, axis=0)
    pooled = call(pool_kernel, shape((VOC, FEAT), jnp.bfloat16), [VMEM, VMEM, VMEM])(
        spread, fetched.reshape(BLOCKS * CAP, FEAT), gain_row
    )

    group = z_ring(pooled, VOC // 2)
    inverse_gain = 1.0 / (gain_row * gain_row)

    def project(extra, weight):
        width = WIDE + (EXTRA if extra else 0)
        return call(
            lambda *refs: project_kernel(extra, *refs),
            [shape((NX, VOC, width), jnp.float32), shape((NX, VOC, width), jnp.bfloat16)],
            [SMEM] + [VMEM] * 11,
            [
                pltpu.VMEM((NZ * VOC, FEAT), jnp.bfloat16),
                pltpu.VMEM((PARTS, VOC, width), jnp.float32),
            ],
        )(place, weight, inverse_gain, *group)

    chip_out = add_core(*project(True, w_out_all), True)
    parts_out = swap(chip_out, "x")
    output_rows, inverse = call(
        norm_kernel,
        [shape((VOC, WIDE), jnp.bfloat16), shape((VOC, 1), jnp.float32)],
        [VMEM],
    )(parts_out)

    first_a, rows_b = 48, VOC - ROWS_A
    near_arrays, near_routes, far_arrays, far_routes = [], [], [], []
    ring_b = y_ring(output_rows[ROWS_A:], 32)
    ring_a = z_ring(output_rows[:ROWS_A], first_a)
    entries_b = pieces_of_stack(y_pieces(rows_b, 32))
    entries_a = z_pieces(ROWS_A, first_a)
    column = jnp.concatenate(ring_b, axis=0)
    height = column.shape[0]
    for array, (dz, low, rows) in zip(z_ring(column, height // 2), z_pieces(height, height // 2)):
        near = abs(dz) < 3
        arrays, routes = (near_arrays, near_routes) if near else (far_arrays, far_routes)
        for dy, at, start, count in overlap(entries_b, low, low + rows):
            routes.append((len(arrays), at, count, dy, dz, ROWS_A + start))
        arrays.append(array)
    for cut, arrays, routes in (
        (slice(0, 5), near_arrays, near_routes),
        (slice(5, 9), far_arrays, far_routes),
    ):
        stack = jnp.concatenate(ring_a[cut], axis=0)
        entries = pieces_of_stack(entries_a[cut])
        height = stack.shape[0]
        half = height // 32 * 16
        for array, (dy, low, rows) in zip(y_ring(stack, half), y_pieces(height, half)):
            for dz, at, start, count in overlap(entries, low, low + rows):
                routes.append((len(arrays), at, count, dy, dz, start))
            arrays.append(array)

    chip_in = add_core(*project(False, after(w_in_all, chip_out)), False)
    parts_in = swap(after(chip_in, output_rows), "x")
    input_rows = call(scale_kernel, shape((NY, VOC, 256), jnp.bfloat16), [VMEM, VMEM])(
        parts_in, inverse
    )
    input_rows = swap(input_rows, "y")
    in_table = lax.all_gather(input_rows, ("x", "c"), axis=0).reshape(BLOCKS * VOC, 256)
    position = ((token_ids >> 7) & 7) * (NY * VOC) + (token_ids >> 10) * VOC + (token_ids & 127)
    embedded = in_table.at[position].get(mode="promise_in_bounds")

    def buffers(shifts, routes):
        return [
            pltpu.VMEM((len(shifts), TOK, WIDE), jnp.bfloat16),
            pltpu.VMEM((len(shifts), NY * VOC, WIDE), jnp.bfloat16),
            pltpu.SemaphoreType.DMA((len(shifts), NY)),
            pltpu.SemaphoreType.DMA((len(routes),)),
        ]

    logits_shape = shape((TOK, NY * VOC), jnp.float32)
    near_shifts, far_shifts = (0, -1, 1, -2, 2), (-3, 3, 4)
    total = call(
        lambda *refs: near_kernel(near_shifts, near_routes, len(near_arrays), *refs),
        logits_shape,
        [SMEM, ANY] + [ANY] * len(near_arrays),
        buffers(near_shifts, near_routes),
        40 * MIB,
    )(place, hidden_all, *near_arrays)
    far_arrays, total, embedded = lax.optimization_barrier((far_arrays, total, embedded))
    stats = call(
        lambda *refs: far_kernel(far_shifts, far_routes, len(far_arrays), *refs),
        shape((PARTS, 8, 128), jnp.float32),
        [SMEM, VMEM, VMEM, ANY] + [ANY] * len(far_arrays),
        [pltpu.VMEM((TOK, NY * VOC), jnp.float32), *buffers(far_shifts, far_routes)],
        40 * MIB,
    )(place, target_column, total, hidden_all, *far_arrays)
    merged = swap(stats, ("x", "c"))
    loss = call(merge_kernel, shape((1, 128), jnp.float32), [VMEM])(merged)
    return (embedded, loss.reshape(128))


def solution(mesh):
    grid = Mesh(mesh.devices.reshape(NY, NZ, NX, NC), ("y", "z", "x", "c"))
    vocab, seq = ("y", "z"), ("x", "c")
    return jax.shard_map(
        on_device,
        mesh=grid,
        in_specs=(
            P(vocab, seq),
            P(vocab, None),
            P(vocab),
            P(),
            P(seq),
            P(seq, vocab),
            P(seq, vocab),
            P(vocab, seq),
            P(seq),
            P(vocab),
        ),
        out_specs=(P(seq, vocab), P((*vocab, *seq))),
        check_vma=False,
    )
```

```python
import jax
import jax.numpy as jnp
from jax import lax
from jax.experimental import pallas as pl
from jax.experimental.pallas import tpu as pltpu
from jax.sharding import Mesh
from jax.sharding import PartitionSpec as P

EPSILON = 1e-05
NY, NZ, NX, NC = 4, 8, 4, 2
BLOCKS = NY * NZ
PARTS = NX * NC
D = 8192
VOC = 128
PIECES = 8
SHARD = 2048
CAP = 32
FEAT = D // PARTS
WIDE = D // NZ
EXTRA = 128
TOK = 1024
HALF = WIDE // 2
MIB = 1 << 20
SHIFTS = (0, 1, 2, -1)

VMEM = pl.BlockSpec(memory_space=pltpu.VMEM)
SMEM = pl.BlockSpec(memory_space=pltpu.SMEM)
ANY = pl.BlockSpec(memory_space=pl.ANY)


def dot(left, right):
    return jnp.dot(left, right, preferred_element_type=jnp.float32)


def dot_dims(left, right, left_dim, right_dim):
    return lax.dot_general(
        left, right, (((left_dim,), (right_dim,)), ((), ())), preferred_element_type=jnp.float32
    )


def call(kernel, out_shape, in_specs, scratch=(), limit=32 * MIB):
    many = isinstance(out_shape, (tuple, list))
    return pl.pallas_call(
        kernel,
        out_shape=out_shape,
        in_specs=in_specs,
        out_specs=[VMEM] * len(out_shape) if many else VMEM,
        scratch_shapes=list(scratch),
        compiler_params=pltpu.CompilerParams(vmem_limit_bytes=limit),
    )


def shape(dims, kind):
    return jax.ShapeDtypeStruct(dims, kind)


def plan_kernel(pieces_ref, lengths_ref, request_ref, where_ref):
    row = lax.broadcasted_iota(jnp.int32, (VOC, VOC), 0)
    col = lax.broadcasted_iota(jnp.int32, (VOC, VOC), 1)
    earlier = (row < col).astype(jnp.float32).astype(jnp.bfloat16)
    level = lax.broadcasted_iota(jnp.int32, (BLOCKS, VOC), 0)
    lengths = lengths_ref[...]
    base = jnp.zeros((BLOCKS, 1), jnp.float32)
    high_sum = jnp.zeros((BLOCKS, CAP), jnp.float32)
    low_sum = jnp.zeros((BLOCKS, CAP), jnp.float32)
    for k in range(PIECES):
        piece = pieces_ref[k : k + 1, :]
        live = lengths > k
        block = jnp.where(live, piece >> 11, BLOCKS)
        local = piece & (SHARD - 1)
        onehot = (block == level).astype(jnp.float32)
        onehot16 = onehot.astype(jnp.bfloat16)
        before = dot(onehot16, earlier) + base
        rank = jnp.sum(before * onehot, axis=0, keepdims=True).astype(jnp.int32)
        base = base + jnp.sum(onehot, axis=1, keepdims=True)
        at_rank = rank == level
        high = jnp.where(at_rank, (local >> 6).astype(jnp.float32), 0.0).astype(jnp.bfloat16)
        low = jnp.where(at_rank, (local & 63).astype(jnp.float32), 0.0).astype(jnp.bfloat16)
        high_sum = high_sum + dot_dims(onehot16, high, 1, 1)
        low_sum = low_sum + dot_dims(onehot16, low, 1, 1)
        where_ref[k : k + 1, :] = jnp.where(live, block * CAP + rank, -1)
    request_ref[...] = high_sum.astype(jnp.int32) * 64 + low_sum.astype(jnp.int32)


def fetch_kernel(wanted_ref, table_ref, out_ref, onehot_buf):
    eye = lax.broadcasted_iota(jnp.int32, (CAP, CAP), 0) == lax.broadcasted_iota(
        jnp.int32, (CAP, CAP), 1
    )
    lane = lax.broadcasted_iota(jnp.int32, (CAP, SHARD), 1)
    half = BLOCKS // 2
    for h in range(2):
        for g in range(half):
            row = wanted_ref[h * half + g].astype(jnp.float32)
            column = jnp.sum(jnp.where(eye, row, 0.0), axis=1, keepdims=True).astype(jnp.int32)
            onehot_buf[h, g * CAP : (g + 1) * CAP, :] = (
                (lane == column).astype(jnp.float32).astype(jnp.bfloat16)
            )
        rows = slice(h * half * CAP, (h + 1) * half * CAP)
        out_ref[rows, :] = dot(onehot_buf[h], table_ref[...]).astype(jnp.bfloat16)


def embed_kernel(position_ref, table_ref, out_ref, onehot_buf):
    tile, count = 512, BLOCKS * VOC
    columns = jnp.concatenate(
        [position_ref[...], jnp.zeros((VOC - count // VOC, VOC), jnp.int32)], axis=0
    ).T
    lane = lax.broadcasted_iota(jnp.int32, (VOC, count), 1)
    for i in range(count // tile):
        for j in range(tile // VOC):
            n = i * (tile // VOC) + j
            onehot_buf[i % 2, j * VOC : (j + 1) * VOC, :] = (
                (lane == columns[:, n : n + 1]).astype(jnp.float32).astype(jnp.bfloat16)
            )
        rows = slice(i * tile, (i + 1) * tile)
        out_ref[rows, :] = dot(onehot_buf[i % 2], table_ref[...]).astype(jnp.bfloat16)


def spread_kernel(gain_ref, where_ref, out_ref):
    lane = lax.broadcasted_iota(jnp.int32, (VOC, BLOCKS * CAP), 1)
    columns = jnp.concatenate(
        [where_ref[...], jnp.zeros((VOC - PIECES, VOC), jnp.int32)], axis=0
    ).T
    total = jnp.zeros((VOC, BLOCKS * CAP), jnp.float32)
    for k in range(PIECES):
        total = jnp.where(columns[:, k : k + 1] == lane, gain_ref[k], total)
    for term in range(3):
        part = total.astype(jnp.bfloat16)
        out_ref[term] = part
        total = total - part.astype(jnp.float32)


def pool_kernel(spread_ref, rows_ref, gain_ref, out_ref):
    rows = rows_ref[...]
    pooled = dot(spread_ref[2], rows) + dot(spread_ref[1], rows) + dot(spread_ref[0], rows)
    out_ref[...] = (pooled * gain_ref[...]).astype(jnp.bfloat16)


def split_two(value, lane):
    high = value.astype(jnp.bfloat16)
    low = (value - high.astype(jnp.float32)).astype(jnp.bfloat16)
    return jnp.where(
        lane == 0, high.astype(jnp.float32), jnp.where(lane == 1, low.astype(jnp.float32), 0.0)
    ).astype(jnp.bfloat16)


def project_kernel(
    extra, place_ref, order_ref, scale_ref, w0, w1, w2, w3, b0, p1, m1, p2, m2, p3, m3, p4, m4,
    keep_ref, give_ref, rows_buf, result_buf, square_buf,
):
    z, core = place_ref[0], place_ref[1]
    blocks = [(0, b0), (-1, p1), (1, m1), (-2, p2), (2, m2), (-3, p3), (3, m3)]
    for step, ref in blocks:
        at = lax.rem(z + (step + NZ), NZ)
        rows_buf[pl.ds(pl.multiple_of(at * VOC, VOC), VOC), :] = ref[...]
    at = lax.rem(z + 4, NZ)
    half = VOC // 2
    rows_buf[pl.ds(pl.multiple_of(at * VOC, half), half), :] = p4[...]
    rows_buf[pl.ds(pl.multiple_of(at * VOC + half, half), half), :] = m4[...]
    for q, weight in enumerate((w0, w1, w2, w3)):
        result_buf[order_ref[q]] = dot(rows_buf[...], weight[...])
    if extra:
        lane = lax.broadcasted_iota(jnp.int32, (VOC, EXTRA), 1)
        scale = scale_ref[...]
        for i in range(PARTS):
            wide = rows_buf[i * VOC : (i + 1) * VOC, :].astype(jnp.float32)
            square = jnp.sum(wide * wide * scale, axis=1, keepdims=True)
            square_buf[i] = split_two(square, lane)
    for i in range(NX):
        mine, other = 2 * i + core, 2 * i + 1 - core
        for q in range(NY):
            columns = slice(q * 256, (q + 1) * 256)
            keep_ref[i, :, columns] = result_buf[q, pl.ds(pl.multiple_of(mine * VOC, VOC), VOC), :]
            give_ref[i, :, columns] = result_buf[
                q, pl.ds(pl.multiple_of(other * VOC, VOC), VOC), :
            ].astype(jnp.bfloat16)
        if extra:
            keep_ref[i, :, WIDE:] = square_buf[mine].astype(jnp.float32)
            give_ref[i, :, WIDE:] = square_buf[other]


def add_kernel(extra, place_ref, keep_ref, got_ref, *out_refs):
    x = place_ref[3] >> 1
    lane = lax.broadcasted_iota(jnp.int32, (VOC, EXTRA), 1)
    for k, out_ref in zip(SHIFTS, out_refs):
        i = lax.rem(x + (k + NX), NX)
        total = keep_ref[i] + got_ref[i].astype(jnp.float32)
        out_ref[:, :WIDE] = total[:, :WIDE].astype(jnp.bfloat16)
        if extra:
            square = jnp.sum(total[:, WIDE:], axis=1, keepdims=True)
            out_ref[:, WIDE:] = split_two(square, lane)


def total_of(refs):
    total = refs[0][...].astype(jnp.float32)
    for ref in refs[1:]:
        total = total + ref[...].astype(jnp.float32)
    return total


def norm_kernel(*refs):
    first_ref, second_ref, inverse_ref = refs[NX:]
    total = total_of(refs[:NX])
    square = jnp.sum(total[:, WIDE:], axis=1, keepdims=True)
    inverse = lax.rsqrt(square / D + EPSILON)
    rows = total[:, :WIDE] * inverse
    first_ref[...] = rows[:, :HALF].T.astype(jnp.bfloat16)
    second_ref[...] = rows[:, HALF:].T.astype(jnp.bfloat16)
    inverse_ref[...] = inverse


def scale_kernel(place_ref, inverse_ref, *refs):
    total = total_of(refs[:NX])
    rows = (total * inverse_ref[...]).astype(jnp.bfloat16)
    for q in range(NY):
        chunk = rows[:, q * 256 : (q + 1) * 256]
        for k, out_ref in zip(SHIFTS, refs[NX:]):

            @pl.when(lax.rem(place_ref[2] + (k + NY), NY) == q)
            def _():
                out_ref[...] = chunk


def shift_by(value, axis, step):
    count = {"y": NY, "z": NZ, "x": NX, "c": NC}[axis]
    return lax.ppermute(value, axis, [(i, (i + step) % count) for i in range(count)])


def z_ring(rows, first):
    p1, m1 = shift_by(rows, "z", 1), shift_by(rows, "z", -1)
    p2, m2 = shift_by(p1, "z", 1), shift_by(m1, "z", -1)
    p3, m3 = shift_by(p2, "z", 1), shift_by(m2, "z", -1)
    p4, m4 = shift_by(p3[:first], "z", 1), shift_by(m3[first:], "z", -1)
    return [rows, p1, m1, p2, m2, p3, m3, p4, m4]


def y_all(block):
    return [block] + [shift_by(block, "y", -step) for step in SHIFTS[1:]]


def deal(blocks, axis):
    return [blocks[0]] + [shift_by(b, axis, k) for b, k in zip(blocks[1:], SHIFTS[1:])]


def accumulate(shifts, routes, arrays, place_ref, hidden_ref, total_ref, bufs):
    hidden_buf, rows_buf, hidden_sem, rows_sem = bufs
    y, z = place_ref[2], place_ref[0]
    waits = [[] for _ in shifts]
    for number, (index, from_row, rows, dy, dz, to_row) in enumerate(routes):
        slot = shifts.index(dz)
        at_y = lax.rem(y + (dy + NY), NY)
        copy = pltpu.make_async_copy(
            arrays[index].at[pl.ds(from_row, rows)],
            rows_buf.at[slot, pl.ds(to_row, rows), pl.ds(pl.multiple_of(at_y * VOC, VOC), VOC)],
            rows_sem.at[number],
        )
        copy.start()
        waits[slot].append(copy)
    for slot, dz in enumerate(shifts):
        at = lax.rem(z + (dz + NZ), NZ)
        for q in range(NY):
            copy = pltpu.make_async_copy(
                hidden_ref.at[2 * q + at // 4, :, pl.ds(pl.multiple_of((at % 4) * 256, 256), 256)],
                hidden_buf.at[slot, :, pl.ds(q * 256, 256)],
                hidden_sem.at[slot, q],
            )
            copy.start()
            waits[slot].append(copy)
    tile = 256
    for slot in range(len(shifts)):
        for copy in waits[slot]:
            copy.wait()
        for i in range(TOK // tile):
            rows = pl.ds(i * tile, tile)
            product = dot(hidden_buf[slot, rows, :], rows_buf[slot])
            total_ref[rows, :] = total_ref[rows, :] + product


def near_kernel(shifts, routes, count, place_ref, hidden_ref, *refs):
    arrays, total_ref = refs[:count], refs[count]
    total_ref[...] = jnp.zeros_like(total_ref)
    accumulate(shifts, routes, arrays, place_ref, hidden_ref, total_ref, refs[count + 1 :])


def far_kernel(shifts, routes, count, place_ref, target_ref, total_in, hidden_ref, *refs):
    arrays, out_ref, total_ref = refs[:count], refs[count], refs[count + 1]
    total_ref[...] = total_in[...]
    accumulate(shifts, routes, arrays, place_ref, hidden_ref, total_ref, refs[count + 2 :])
    part = place_ref[3]
    tile = 256
    column = lax.broadcasted_iota(jnp.int32, (tile, NY * VOC), 1)
    token_of = (column // VOC) * (NZ * VOC) + part * VOC + column % VOC
    lane = lax.broadcasted_iota(jnp.int32, (tile, 128), 1)
    for i in range(TOK // tile):
        rows = pl.ds(i * tile, tile)
        total = total_ref[rows, :]
        best = jnp.max(total, axis=1, keepdims=True)
        spread = jnp.sum(jnp.exp(total - best), axis=1, keepdims=True)
        hit = jnp.sum(jnp.where(token_of == target_ref[rows, :], total, 0.0), axis=1, keepdims=True)
        packed = jnp.where(lane == 0, best, jnp.where(lane == 1, spread, hit))
        turned = packed.T
        for j in range(tile // 128):
            out_ref[i * (tile // 128) + j] = turned[:8, j * 128 : (j + 1) * 128]


def merge_kernel(parts_ref, out_ref):
    best = parts_ref[0, 0:1, :]
    for i in range(1, PARTS):
        best = jnp.maximum(best, parts_ref[i, 0:1, :])
    spread = jnp.zeros_like(best)
    hit = jnp.zeros_like(best)
    for i in range(PARTS):
        spread = spread + parts_ref[i, 1:2, :] * jnp.exp(parts_ref[i, 0:1, :] - best)
        hit = hit + parts_ref[i, 2:3, :]
    out_ref[...] = best + jnp.log(spread) - hit


def add_core(place, keep, give, extra):
    got = shift_by(give, "c", 1)
    return call(
        lambda *refs: add_kernel(extra, *refs),
        [shape(keep.shape[1:], jnp.bfloat16)] * NX,
        [SMEM, VMEM, VMEM],
    )(place, keep, got)


def swap(value, axes):
    return lax.all_to_all(value, axes, split_axis=0, concat_axis=0, tiled=True)


def after(value, *others):
    return lax.optimization_barrier((value, *others))[0]


def on_device(
    old_table, pieces, lengths, pos_gain, hyp_gain, w_in, w_out, hidden, token_ids, targets
):
    y, z = lax.axis_index("y"), lax.axis_index("z")
    core = lax.axis_index("c")
    part = lax.axis_index(("x", "c"))
    place = jnp.stack([z, core, y, part]).astype(jnp.int32)
    gain_row = hyp_gain.reshape(1, FEAT)
    target_column = targets.reshape(TOK, 1)

    hidden_all = lax.all_gather(hidden, ("x", "c"), axis=0)
    w_in_all = lax.all_gather(after(w_in, hidden_all), "y", axis=0)

    requests, where = call(
        plan_kernel,
        [shape((BLOCKS, CAP), jnp.int32), shape((PIECES, VOC), jnp.int32)],
        [VMEM, VMEM],
    )(pieces.T, lengths.reshape(1, VOC))
    wanted = swap(requests.reshape(BLOCKS, 1, CAP), ("y", "z"))
    found = call(
        fetch_kernel,
        shape((BLOCKS * CAP, FEAT), jnp.bfloat16),
        [VMEM, VMEM],
        [pltpu.VMEM((2, BLOCKS * CAP // 2, SHARD), jnp.bfloat16)],
    )(wanted, old_table)
    fetched = swap(found.reshape(BLOCKS, CAP, FEAT), ("y", "z"))
    spread = call(
        spread_kernel, shape((3, VOC, BLOCKS * CAP), jnp.bfloat16), [SMEM, VMEM]
    )(pos_gain, where)
    w_out_all = y_all(after(w_out, found))
    fetched, *w_out_all = lax.optimization_barrier((fetched, *w_out_all))
    pooled = call(pool_kernel, shape((VOC, FEAT), jnp.bfloat16), [VMEM, VMEM, VMEM])(
        spread, fetched.reshape(BLOCKS * CAP, FEAT), gain_row
    )

    group = z_ring(pooled, VOC // 2)
    inverse_gain = 1.0 / (gain_row * gain_row)

    def project(extra, order, weights):
        width = WIDE + (EXTRA if extra else 0)
        return call(
            lambda *refs: project_kernel(extra, *refs),
            [shape((NX, VOC, width), jnp.float32), shape((NX, VOC, width), jnp.bfloat16)],
            [SMEM, SMEM] + [VMEM] * 14,
            [
                pltpu.VMEM((NZ * VOC, FEAT), jnp.bfloat16),
                pltpu.VMEM((NY, NZ * VOC, 256), jnp.float32),
                pltpu.VMEM((PARTS, VOC, EXTRA), jnp.bfloat16),
            ],
        )(place, order, inverse_gain, *weights, *group)

    near_y = (y + jnp.array(SHIFTS, jnp.int32)) % NY
    chip_out = add_core(place, *project(True, near_y, w_out_all), True)
    out_parts = deal(chip_out, "x")
    first_half, second_half, inverse = call(
        norm_kernel,
        [shape((HALF, VOC), jnp.bfloat16)] * 2 + [shape((VOC, 1), jnp.float32)],
        [VMEM] * NX,
    )(*out_parts)

    near_arrays, near_routes, far_arrays, far_routes = [], [], [], []
    ring_z = z_ring(first_half, HALF // 2)
    column = after(jnp.concatenate(y_all(second_half), axis=0), *ring_z[1:3])
    ring_b = z_ring(column, 2 * HALF)
    entries = [(dy, i * HALF, HALF, HALF) for i, dy in enumerate(SHIFTS)]
    for dz, array in zip((0, -1, 1, -2, 2, -3, 3), ring_b):
        arrays, routes = (near_arrays, near_routes) if abs(dz) < 3 else (far_arrays, far_routes)
        for dy, at, to_row, count in entries:
            routes.append((len(arrays), at, count, dy, dz, to_row))
        arrays.append(array)
    for part_of, array in enumerate(ring_b[7:]):
        for dy, at, to_row, count in entries[2 * part_of : 2 * part_of + 2]:
            far_routes.append((len(far_arrays), at - part_of * 2 * HALF, count, dy, 4, to_row))
        far_arrays.append(array)
    pieces_a = [(dz, 0, HALF) for dz in (0, -1, 1, -2, 2, -3, 3)]
    pieces_a += [(4, 0, HALF // 2), (4, HALF // 2, HALF // 2)]
    for cut, arrays, routes in (
        (slice(0, 5), near_arrays, near_routes),
        (slice(5, 9), far_arrays, far_routes),
    ):
        stack = jnp.concatenate(ring_z[cut], axis=0)
        for dy, array in zip(SHIFTS, y_all(stack)):
            at = 0
            for dz, to_row, count in pieces_a[cut]:
                routes.append((len(arrays), at, count, dy, dz, to_row))
                at += count
            arrays.append(array)

    absolute = jnp.arange(NY, dtype=jnp.int32)
    in_weights = after(w_in_all, out_parts[1])
    in_parts = project(False, absolute, [in_weights[q] for q in range(NY)])
    chip_in = add_core(place, *in_parts, False)
    chip_in = lax.optimization_barrier((chip_in, column, ring_z[3:5]))[0]
    input_rows = call(
        scale_kernel, [shape((VOC, 256), jnp.bfloat16)] * NY, [SMEM, VMEM] + [VMEM] * NX
    )(place, inverse, *deal(chip_in, "x"))
    input_rows = jnp.concatenate(deal(input_rows, "y"), axis=0)
    in_table = lax.all_gather(input_rows, ("x", "c"), axis=0).reshape(BLOCKS * VOC, 256)
    back = (y - (token_ids >> 10)) & 3
    position = ((token_ids >> 7) & 7) * (NY * VOC) + back * VOC + (token_ids & 127)
    embedded = call(
        embed_kernel,
        shape((BLOCKS * VOC, 256), jnp.bfloat16),
        [VMEM, VMEM],
        [pltpu.VMEM((2, 512, BLOCKS * VOC), jnp.bfloat16)],
    )(position.reshape(-1, VOC), in_table)

    def buffers(shifts, routes):
        return [
            pltpu.VMEM((len(shifts), TOK, WIDE), jnp.bfloat16),
            pltpu.VMEM((len(shifts), WIDE, NY * VOC), jnp.bfloat16),
            pltpu.SemaphoreType.DMA((len(shifts), NY)),
            pltpu.SemaphoreType.DMA((len(routes),)),
        ]

    logits_shape = shape((TOK, NY * VOC), jnp.float32)
    near_shifts, far_shifts = (0, -1, 1, -2, 2), (-3, 3, 4)
    total = call(
        lambda *refs: near_kernel(near_shifts, near_routes, len(near_arrays), *refs),
        logits_shape,
        [SMEM, ANY] + [ANY] * len(near_arrays),
        buffers(near_shifts, near_routes),
        40 * MIB,
    )(place, hidden_all, *near_arrays)
    far_arrays, total, embedded = lax.optimization_barrier((far_arrays, total, embedded))
    stats = call(
        lambda *refs: far_kernel(far_shifts, far_routes, len(far_arrays), *refs),
        shape((PARTS, 8, 128), jnp.float32),
        [SMEM, VMEM, VMEM, ANY] + [ANY] * len(far_arrays),
        [pltpu.VMEM((TOK, NY * VOC), jnp.float32), *buffers(far_shifts, far_routes)],
        40 * MIB,
    )(place, target_column, total, hidden_all, *far_arrays)
    merged = swap(stats, ("x", "c"))
    loss = call(merge_kernel, shape((1, 128), jnp.float32), [VMEM])(merged)
    return (embedded, loss.reshape(128))


def solution(mesh):
    grid = Mesh(mesh.devices.reshape(NY, NZ, NX, NC), ("y", "z", "x", "c"))
    vocab, seq = ("y", "z"), ("x", "c")
    return jax.shard_map(
        on_device,
        mesh=grid,
        in_specs=(
            P(vocab, seq),
            P(vocab, None),
            P(vocab),
            P(),
            P(seq),
            P(seq, vocab),
            P(seq, vocab),
            P(vocab, seq),
            P(seq),
            P(vocab),
        ),
        out_specs=(P(seq, vocab), P((*vocab, *seq))),
        check_vma=False,
    )
```

```python
import jax
import jax.numpy as jnp
from jax import lax
from jax.experimental import pallas as pl
from jax.experimental.pallas import tpu as pltpu
from jax.sharding import Mesh
from jax.sharding import PartitionSpec as P

EPSILON = 1e-05
NY, NZ, NX, NC = 4, 8, 4, 2
BLOCKS = NY * NZ
PARTS = NX * NC
D = 8192
VOC = 128
PIECES = 8
SHARD = 2048
CAP = 32
FEAT = D // PARTS
WIDE = D // NZ
EXTRA = 128
TOK = 1024
HALF = WIDE // 2
MIB = 1 << 20
MOST = 56 * MIB
SHIFTS = (0, 1, 2, -1)

VMEM = pl.BlockSpec(memory_space=pltpu.VMEM)
SMEM = pl.BlockSpec(memory_space=pltpu.SMEM)
ANY = pl.BlockSpec(memory_space=pltpu.HBM)


def dot(left, right):
    return jnp.dot(left, right, preferred_element_type=jnp.float32)


def dot_dims(left, right, left_dim, right_dim):
    return lax.dot_general(
        left, right, (((left_dim,), (right_dim,)), ((), ())), preferred_element_type=jnp.float32
    )


def call(kernel, out_shape, in_specs, scratch=(), limit=16 * MIB):
    many = isinstance(out_shape, (tuple, list))
    return pl.pallas_call(
        kernel,
        out_shape=out_shape,
        in_specs=in_specs,
        out_specs=[VMEM] * len(out_shape) if many else VMEM,
        scratch_shapes=list(scratch),
        compiler_params=pltpu.CompilerParams(vmem_limit_bytes=limit),
    )


def shape(dims, kind):
    return jax.ShapeDtypeStruct(dims, kind)


def plan_kernel(pieces_ref, lengths_ref, request_ref, where_ref):
    row = lax.broadcasted_iota(jnp.int32, (VOC, VOC), 0)
    col = lax.broadcasted_iota(jnp.int32, (VOC, VOC), 1)
    earlier = (row < col).astype(jnp.float32).astype(jnp.bfloat16)
    level = lax.broadcasted_iota(jnp.int32, (BLOCKS, VOC), 0)
    lengths = lengths_ref[...]
    base = jnp.zeros((BLOCKS, 1), jnp.float32)
    high_sum = jnp.zeros((BLOCKS, CAP), jnp.float32)
    low_sum = jnp.zeros((BLOCKS, CAP), jnp.float32)
    for k in range(PIECES):
        piece = pieces_ref[k : k + 1, :]
        live = lengths > k
        block = jnp.where(live, piece >> 11, BLOCKS)
        local = piece & (SHARD - 1)
        onehot = (block == level).astype(jnp.float32)
        onehot16 = onehot.astype(jnp.bfloat16)
        before = dot(onehot16, earlier) + base
        rank = jnp.sum(before * onehot, axis=0, keepdims=True).astype(jnp.int32)
        base = base + jnp.sum(onehot, axis=1, keepdims=True)
        at_rank = rank == level
        high = jnp.where(at_rank, (local >> 6).astype(jnp.float32), 0.0).astype(jnp.bfloat16)
        low = jnp.where(at_rank, (local & 63).astype(jnp.float32), 0.0).astype(jnp.bfloat16)
        high_sum = high_sum + dot_dims(onehot16, high, 1, 1)
        low_sum = low_sum + dot_dims(onehot16, low, 1, 1)
        where_ref[k : k + 1, :] = jnp.where(live, block * CAP + rank, -1)
    request_ref[...] = high_sum.astype(jnp.int32) * 64 + low_sum.astype(jnp.int32)


def fetch_kernel(wanted_ref, table_ref, out_ref, onehot_buf, table_buf, sem):
    copy = pltpu.make_async_copy(table_ref, table_buf, sem)
    copy.start()
    eye = lax.broadcasted_iota(jnp.int32, (CAP, CAP), 0) == lax.broadcasted_iota(
        jnp.int32, (CAP, CAP), 1
    )
    lane = lax.broadcasted_iota(jnp.int32, (CAP, SHARD), 1)
    half = BLOCKS // 2
    for h in range(2):
        for g in range(half):
            row = wanted_ref[h * half + g].astype(jnp.float32)
            column = jnp.sum(jnp.where(eye, row, 0.0), axis=1, keepdims=True).astype(jnp.int32)
            onehot_buf[h, g * CAP : (g + 1) * CAP, :] = (
                (lane == column).astype(jnp.float32).astype(jnp.bfloat16)
            )
        if h == 0:
            copy.wait()
        rows = slice(h * half * CAP, (h + 1) * half * CAP)
        out_ref[rows, :] = dot(onehot_buf[h], table_buf[...]).astype(jnp.bfloat16)


def embed_kernel(position_ref, table_ref, out_ref, onehot_buf):
    tile, count = 512, BLOCKS * VOC
    columns = jnp.concatenate(
        [position_ref[...], jnp.zeros((VOC - count // VOC, VOC), jnp.int32)], axis=0
    ).T
    lane = lax.broadcasted_iota(jnp.int32, (VOC, count), 1)
    for i in range(count // tile):
        for j in range(tile // VOC):
            n = i * (tile // VOC) + j
            onehot_buf[i % 2, j * VOC : (j + 1) * VOC, :] = (
                (lane == columns[:, n : n + 1]).astype(jnp.float32).astype(jnp.bfloat16)
            )
        rows = slice(i * tile, (i + 1) * tile)
        out_ref[rows, :] = dot(onehot_buf[i % 2], table_ref[...]).astype(jnp.bfloat16)


def spread_kernel(gain_ref, where_ref, out_ref):
    lane = lax.broadcasted_iota(jnp.int32, (VOC, BLOCKS * CAP), 1)
    columns = jnp.concatenate(
        [where_ref[...], jnp.zeros((VOC - PIECES, VOC), jnp.int32)], axis=0
    ).T
    total = jnp.zeros((VOC, BLOCKS * CAP), jnp.float32)
    for k in range(PIECES):
        total = jnp.where(columns[:, k : k + 1] == lane, gain_ref[k], total)
    for term in range(3):
        part = total.astype(jnp.bfloat16)
        out_ref[term] = part
        total = total - part.astype(jnp.float32)


def pool_kernel(spread_ref, rows_ref, gain_ref, out_ref):
    rows = rows_ref[...]
    pooled = dot(spread_ref[2], rows) + dot(spread_ref[1], rows) + dot(spread_ref[0], rows)
    out_ref[...] = (pooled * gain_ref[...]).astype(jnp.bfloat16)


def split_two(value, lane):
    high = value.astype(jnp.bfloat16)
    low = (value - high.astype(jnp.float32)).astype(jnp.bfloat16)
    return jnp.where(
        lane == 0, high.astype(jnp.float32), jnp.where(lane == 1, low.astype(jnp.float32), 0.0)
    ).astype(jnp.bfloat16)


def gather_rows(place_ref, refs, rows_buf):
    z = place_ref[0]
    for step, ref in zip((0, -1, 1, -2, 2, -3, 3), refs):
        at = lax.rem(z + (step + NZ), NZ)
        rows_buf[pl.ds(pl.multiple_of(at * VOC, VOC), VOC), :] = ref[...]
    at = lax.rem(z + 4, NZ)
    half = VOC // 2
    rows_buf[pl.ds(pl.multiple_of(at * VOC, half), half), :] = refs[7][...]
    rows_buf[pl.ds(pl.multiple_of(at * VOC + half, half), half), :] = refs[8][...]


def project_out_kernel(place_ref, order_ref, scale_ref, *refs):
    keep_ref, give_ref, rows_buf, result_buf, square_buf = refs[-5:]
    core = place_ref[1]
    gather_rows(place_ref, refs[:9], rows_buf)
    for q in range(NY):
        result_buf[order_ref[q]] = dot(rows_buf[...], refs[9][q])
    lane = lax.broadcasted_iota(jnp.int32, (VOC, EXTRA), 1)
    scale = scale_ref[...]
    for i in range(PARTS):
        wide = rows_buf[i * VOC : (i + 1) * VOC, :].astype(jnp.float32)
        square = jnp.sum(wide * wide * scale, axis=1, keepdims=True)
        square_buf[i] = split_two(square, lane)
    for i in range(NX):
        mine, other = 2 * i + core, 2 * i + 1 - core
        for q in range(NY):
            columns = slice(q * 256, (q + 1) * 256)
            keep_ref[i, :, columns] = result_buf[q, pl.ds(pl.multiple_of(mine * VOC, VOC), VOC), :]
            give_ref[i, :, columns] = result_buf[
                q, pl.ds(pl.multiple_of(other * VOC, VOC), VOC), :
            ].astype(jnp.bfloat16)
        keep_ref[i, :, WIDE:] = square_buf[mine].astype(jnp.float32)
        give_ref[i, :, WIDE:] = square_buf[other]


def project_in_kernel(place_ref, *refs):
    weight_ref, out_ref, rows_buf = refs[-3:]
    gather_rows(place_ref, refs[:9], rows_buf)
    for q in range(NY):
        out_ref[:, q * 256 : (q + 1) * 256] = dot(rows_buf[...], weight_ref[q])


def add_kernel(place_ref, keep_ref, got_ref, *out_refs):
    x = place_ref[3] >> 1
    lane = lax.broadcasted_iota(jnp.int32, (VOC, EXTRA), 1)
    for k, out_ref in zip(SHIFTS, out_refs):
        i = lax.rem(x + (k + NX), NX)
        total = keep_ref[i] + got_ref[i].astype(jnp.float32)
        out_ref[:, :WIDE] = total[:, :WIDE].astype(jnp.bfloat16)
        square = jnp.sum(total[:, WIDE:], axis=1, keepdims=True)
        out_ref[:, WIDE:] = split_two(square, lane)


def total_of(refs):
    total = refs[0][...].astype(jnp.float32)
    for ref in refs[1:]:
        total = total + ref[...].astype(jnp.float32)
    return total


def norm_kernel(*refs):
    first_ref, second_ref, inverse_ref = refs[NX:]
    total = total_of(refs[:NX])
    square = jnp.sum(total[:, WIDE:], axis=1, keepdims=True)
    inverse = lax.rsqrt(square / D + EPSILON)
    rows = total[:, :WIDE] * inverse
    first_ref[...] = rows[:, :HALF].T.astype(jnp.bfloat16)
    second_ref[...] = rows[:, HALF:].T.astype(jnp.bfloat16)
    inverse_ref[...] = inverse


def scale_kernel(place_ref, inverse_ref, total_ref, *out_refs):
    rows = (total_ref[...] * inverse_ref[...]).astype(jnp.bfloat16)
    for q in range(NY):
        for k, out_ref in zip(SHIFTS, out_refs):

            @pl.when(lax.rem(place_ref[2] + (k + NY), NY) == q)
            def _():
                out_ref[:VOC, :] = rows[:, q * 256 : q * 256 + VOC]
                out_ref[VOC:, :] = rows[:, q * 256 + VOC : (q + 1) * 256]


def shift_by(value, axis, step):
    count = {"y": NY, "z": NZ, "x": NX, "c": NC}[axis]
    return lax.ppermute(value, axis, [(i, (i + step) % count) for i in range(count)])


def z_ring(rows, first):
    p1, m1 = shift_by(rows, "z", 1), shift_by(rows, "z", -1)
    p2, m2 = shift_by(p1, "z", 1), shift_by(m1, "z", -1)
    p3, m3 = shift_by(p2, "z", 1), shift_by(m2, "z", -1)
    p4, m4 = shift_by(p3[:first], "z", 1), shift_by(m3[first:], "z", -1)
    return [rows, p1, m1, p2, m2, p3, m3, p4, m4]


def y_all(block):
    return [block] + [shift_by(block, "y", -step) for step in SHIFTS[1:]]


def deal(blocks, axis):
    return [blocks[0]] + [shift_by(b, axis, k) for b, k in zip(blocks[1:], SHIFTS[1:])]


def accumulate(shifts, routes, arrays, place_ref, hidden_ref, total_ref, bufs):
    hidden_buf, rows_buf, hidden_sem, rows_sem = bufs
    y, z = place_ref[2], place_ref[0]
    waits = [[] for _ in shifts]
    for slot, step in enumerate(shifts):
        at = lax.rem(z + (step + NZ), NZ)
        for q in range(NY):
            copy = pltpu.make_async_copy(
                hidden_ref.at[2 * q + at // 4, :, pl.ds(pl.multiple_of((at % 4) * 256, 256), 256)],
                hidden_buf.at[slot, :, pl.ds(q * 256, 256)],
                hidden_sem.at[slot, q],
            )
            copy.start()
            waits[slot].append(copy)
        for number, (index, from_row, rows, dy, dz, to_row) in enumerate(routes):
            if dz != step:
                continue
            at_y = lax.rem(y + (dy + NY), NY)
            copy = pltpu.make_async_copy(
                arrays[index].at[pl.ds(from_row, rows)],
                rows_buf.at[slot, pl.ds(to_row, rows), pl.ds(pl.multiple_of(at_y * VOC, VOC), VOC)],
                rows_sem.at[number],
            )
            copy.start()
            waits[slot].append(copy)
    tile = 256
    for slot in range(len(shifts)):
        for copy in waits[slot]:
            copy.wait()
        for i in range(TOK // tile):
            rows = pl.ds(i * tile, tile)
            product = dot(hidden_buf[slot, rows, :], rows_buf[slot])
            total_ref[rows, :] = total_ref[rows, :] + product


def near_kernel(shifts, routes, count, place_ref, hidden_ref, *refs):
    arrays, total_ref = refs[:count], refs[count]
    total_ref[...] = jnp.zeros_like(total_ref)
    accumulate(shifts, routes, arrays, place_ref, hidden_ref, total_ref, refs[count + 1 :])


def middle_kernel(shifts, routes, count, place_ref, total_in, hidden_ref, *refs):
    arrays, total_ref = refs[:count], refs[count]
    total_ref[...] = total_in[...]
    accumulate(shifts, routes, arrays, place_ref, hidden_ref, total_ref, refs[count + 1 :])


def far_kernel(shifts, routes, count, place_ref, target_ref, total_in, hidden_ref, *refs):
    arrays, out_ref, total_ref = refs[:count], refs[count], refs[count + 1]
    total_ref[...] = total_in[...]
    accumulate(shifts, routes, arrays, place_ref, hidden_ref, total_ref, refs[count + 2 :])
    part = place_ref[3]
    tile = 256
    column = lax.broadcasted_iota(jnp.int32, (tile, NY * VOC), 1)
    token_of = (column // VOC) * (NZ * VOC) + part * VOC + column % VOC
    lane = lax.broadcasted_iota(jnp.int32, (tile, 128), 1)
    for i in range(TOK // tile):
        rows = pl.ds(i * tile, tile)
        total = total_ref[rows, :]
        best = jnp.max(total, axis=1, keepdims=True)
        spread = jnp.sum(jnp.exp(total - best), axis=1, keepdims=True)
        hit = jnp.sum(jnp.where(token_of == target_ref[rows, :], total, 0.0), axis=1, keepdims=True)
        packed = jnp.where(lane == 0, best, jnp.where(lane == 1, spread, hit))
        turned = packed.T
        for j in range(tile // 128):
            out_ref[i * (tile // 128) + j] = turned[:8, j * 128 : (j + 1) * 128]


def merge_kernel(parts_ref, out_ref):
    best = parts_ref[0, 0:1, :]
    for i in range(1, PARTS):
        best = jnp.maximum(best, parts_ref[i, 0:1, :])
    spread = jnp.zeros_like(best)
    hit = jnp.zeros_like(best)
    for i in range(PARTS):
        spread = spread + parts_ref[i, 1:2, :] * jnp.exp(parts_ref[i, 0:1, :] - best)
        hit = hit + parts_ref[i, 2:3, :]
    out_ref[...] = best + jnp.log(spread) - hit


def swap(value, axes):
    return lax.all_to_all(value, axes, split_axis=0, concat_axis=0, tiled=True)


def after(value, *others):
    return lax.optimization_barrier((value, *others))[0]


def on_device(
    old_table, pieces, lengths, pos_gain, hyp_gain, w_in, w_out, hidden, token_ids, targets
):
    y, z = lax.axis_index("y"), lax.axis_index("z")
    core = lax.axis_index("c")
    part = lax.axis_index(("x", "c"))
    place = jnp.stack([z, core, y, part]).astype(jnp.int32)
    gain_row = hyp_gain.reshape(1, FEAT)
    target_column = targets.reshape(TOK, 1)

    hidden_all = lax.all_gather(hidden, ("x", "c"), axis=0)

    requests, where = call(
        plan_kernel,
        [shape((BLOCKS, CAP), jnp.int32), shape((PIECES, VOC), jnp.int32)],
        [VMEM, VMEM],
    )(pieces.T, lengths.reshape(1, VOC))
    wanted = swap(requests.reshape(BLOCKS, 1, CAP), ("y", "z"))
    found = call(
        fetch_kernel,
        shape((BLOCKS * CAP, FEAT), jnp.bfloat16),
        [VMEM, ANY],
        [
            pltpu.VMEM((2, BLOCKS * CAP // 2, SHARD), jnp.bfloat16),
            pltpu.VMEM((SHARD, FEAT), jnp.bfloat16),
            pltpu.SemaphoreType.DMA(()),
        ],
        MOST,
    )(wanted, old_table)
    fetched = swap(found.reshape(BLOCKS, CAP, FEAT), ("y", "z"))
    spread = call(
        spread_kernel, shape((3, VOC, BLOCKS * CAP), jnp.bfloat16), [SMEM, VMEM]
    )(pos_gain, where)
    w_in_all = lax.all_gather(after(w_in, found), "y", axis=0)
    w_out_all = y_all(after(w_out, found))
    fetched, w_out_all = lax.optimization_barrier((fetched, jnp.stack(w_out_all)))
    pooled = call(pool_kernel, shape((VOC, FEAT), jnp.bfloat16), [VMEM, VMEM, VMEM])(
        spread, fetched.reshape(BLOCKS * CAP, FEAT), gain_row
    )

    group = z_ring(pooled, VOC // 2)
    inverse_gain = 1.0 / (gain_row * gain_row)

    order = (y + jnp.array(SHIFTS, jnp.int32)) % NY
    w_out_all, hidden_all = lax.optimization_barrier((w_out_all, hidden_all))
    wider = WIDE + EXTRA
    keep, give = call(
        project_out_kernel,
        [shape((NX, VOC, wider), jnp.float32), shape((NX, VOC, wider), jnp.bfloat16)],
        [SMEM, SMEM] + [VMEM] * 11,
        [
            pltpu.VMEM((NZ * VOC, FEAT), jnp.bfloat16),
            pltpu.VMEM((NY, NZ * VOC, 256), jnp.float32),
            pltpu.VMEM((PARTS, VOC, EXTRA), jnp.bfloat16),
        ],
    )(place, order, inverse_gain, *group, w_out_all)
    chip_out = call(
        add_kernel, [shape((VOC, wider), jnp.bfloat16)] * NX, [SMEM, VMEM, VMEM]
    )(place, keep, shift_by(give, "c", 1))
    first_half, second_half, inverse = call(
        norm_kernel,
        [shape((HALF, VOC), jnp.bfloat16)] * 2 + [shape((VOC, 1), jnp.float32)],
        [VMEM] * NX,
    )(*deal(chip_out, "x"))

    def step(pair):
        return [shift_by(pair[0], "z", 1), shift_by(pair[1], "z", -1)]

    def tie(*values):
        return lax.optimization_barrier(values)

    first_half, second_half, w_in_all = tie(first_half, second_half, w_in_all)
    partial_in = call(
        project_in_kernel,
        shape((NZ * VOC, WIDE), jnp.float32),
        [SMEM] + [VMEM] * 10,
        [pltpu.VMEM((NZ * VOC, FEAT), jnp.bfloat16)],
    )(place, *group, w_in_all)
    a1, own_y, partial_in = tie(
        step([first_half, first_half]), y_all(second_half), partial_in
    )
    total_in = lax.psum_scatter(partial_in, ("x", "c"), scatter_dimension=0, tiled=True)
    column = jnp.concatenate(own_y, axis=0)
    pair_1 = [jnp.concatenate([a, column], axis=0) for a in a1]
    stack_1 = jnp.concatenate([first_half, *a1], axis=0)

    pair_1, stack_1 = tie(pair_1, stack_1)
    pair_2, ring_1 = tie(step(pair_1), y_all(stack_1))

    pair_2, stack_2 = tie(pair_2, jnp.concatenate([m[:HALF] for m in pair_2], axis=0))
    pair_3, ring_2 = tie(step(pair_2), y_all(stack_2))

    input_rows = call(
        scale_kernel, [shape((256, VOC), jnp.bfloat16)] * NY, [SMEM, VMEM, VMEM]
    )(place, inverse, total_in)
    stack_3 = [m[:HALF] for m in pair_3]
    stacks = [jnp.concatenate([*stack_3, chunk], axis=0) for chunk in input_rows]
    pair_3, stacks = tie(pair_3, stacks)
    def take(kind, array, entries):
        for entry in entries:
            kind[1].append((len(kind[0]), *entry))
        kind[0].append(array)

    def column_at(low, dz):
        return [(low + i * HALF, HALF, dy, dz, HALF) for i, dy in enumerate(SHIFTS)]

    def others(shifts, arrays):
        return list(zip(shifts, arrays))[1:]

    def buffers(shifts, routes):
        return [
            pltpu.VMEM((len(shifts), TOK, WIDE), jnp.bfloat16),
            pltpu.VMEM((len(shifts), WIDE, NY * VOC), jnp.bfloat16),
            pltpu.SemaphoreType.DMA((len(shifts), NY)),
            pltpu.SemaphoreType.DMA((len(routes),)),
        ]

    near, middle, far = ([], []), ([], []), ([], [])
    take(near, column, column_at(0, 0))
    take(near, first_half, [(0, HALF, 0, 0, 0)])
    for a, dz in zip(a1, (-1, 1)):
        take(near, a, [(0, HALF, 0, dz, 0)])
    for m, dz in zip(pair_2, (-1, 1)):
        take(near, m, [(0, HALF, 0, 2 * dz, 0), *column_at(HALF, dz)])
    for m, dz in zip(pair_3, (-1, 1)):
        take(near, m, column_at(HALF, 2 * dz))
    for dy, array in others(SHIFTS, ring_1):
        take(near, array, [(i * HALF, HALF, dy, dz, 0) for i, dz in enumerate((0, -1, 1))])
    for dy, array in others(SHIFTS, ring_2):
        take(near, array, [(i * HALF, HALF, dy, dz, 0) for i, dz in enumerate((-2, 2))])

    logits_shape = shape((TOK, NY * VOC), jnp.float32)
    near_shifts, middle_shifts, far_shifts = (0, -1, 1, -2, 2), (-3, 3), (4,)
    total = call(
        lambda *refs: near_kernel(near_shifts, near[1], len(near[0]), *refs),
        logits_shape,
        [SMEM, ANY] + [ANY] * len(near[0]),
        buffers(near_shifts, near[1]),
        MOST,
    )(place, hidden_all, *near[0])
    pair_4, ring_3, total = tie(step(pair_3), deal(stacks, "y"), total)
    chunks = [array[2 * HALF :] for array in ring_3]
    chunks = [jnp.concatenate([c[:VOC], c[VOC:]], axis=1) for c in chunks]
    in_table = lax.all_gather(jnp.concatenate(chunks, axis=0), ("x", "c"), axis=0)

    for m, dz in zip(pair_3, (-1, 1)):
        take(middle, m, [(0, HALF, 0, 3 * dz, 0)])
    for m, dz in zip(pair_4, (-1, 1)):
        take(middle, m, column_at(HALF, 3 * dz))
    for dy, array in others([-k for k in SHIFTS], ring_3):
        take(middle, array, [(i * HALF, HALF, dy, dz, 0) for i, dz in enumerate((-3, 3))])
    last_a, last_b = pair_4[1][:HALF], [pair_4[0][HALF : 3 * HALF], pair_4[1][3 * HALF :]]
    take(far, last_a, [(0, HALF, 0, 4, 0)])
    last_a, last_b, total = tie(last_a, last_b, total)
    total = call(
        lambda *refs: middle_kernel(middle_shifts, middle[1], len(middle[0]), *refs),
        logits_shape,
        [SMEM, VMEM, ANY] + [ANY] * len(middle[0]),
        buffers(middle_shifts, middle[1]),
        MOST,
    )(place, total, hidden_all, *middle[0])
    last_z, last_y, total = tie(step(last_b), y_all(last_a), total)
    for dy, array in others(SHIFTS, last_y):
        take(far, array, [(0, HALF, dy, 4, 0)])
    for half, array in enumerate(last_z):
        dys = SHIFTS[2 * half : 2 * half + 2]
        take(far, array, [(i * HALF, HALF, dy, 4, HALF) for i, dy in enumerate(dys)])

    back = (y - (token_ids >> 10)) & 3
    position = ((token_ids >> 7) & 7) * (NY * VOC) + back * VOC + (token_ids & 127)
    embedded = call(
        embed_kernel,
        shape((BLOCKS * VOC, 256), jnp.bfloat16),
        [VMEM, VMEM],
        [pltpu.VMEM((2, 512, BLOCKS * VOC), jnp.bfloat16)],
        20 * MIB,
    )(position.reshape(-1, VOC), in_table.reshape(BLOCKS * VOC, 256))

    stats = call(
        lambda *refs: far_kernel(far_shifts, far[1], len(far[0]), *refs),
        shape((PARTS, 8, 128), jnp.float32),
        [SMEM, VMEM, VMEM, ANY] + [ANY] * len(far[0]),
        [pltpu.VMEM((TOK, NY * VOC), jnp.float32), *buffers(far_shifts, far[1])],
        MOST,
    )(place, target_column, total, hidden_all, *far[0])
    merged, embedded = tie(swap(stats, ("x", "c")), embedded)
    loss = call(merge_kernel, shape((1, 128), jnp.float32), [VMEM])(merged)
    return (embedded, loss.reshape(128))


def solution(mesh):
    grid = Mesh(mesh.devices.reshape(NY, NZ, NX, NC), ("y", "z", "x", "c"))
    vocab, seq = ("y", "z"), ("x", "c")
    return jax.shard_map(
        on_device,
        mesh=grid,
        in_specs=(
            P(vocab, seq),
            P(vocab, None),
            P(vocab),
            P(),
            P(seq),
            P(seq, vocab),
            P(seq, vocab),
            P(vocab, seq),
            P(seq),
            P(vocab),
        ),
        out_specs=(P(seq, vocab), P((*vocab, *seq))),
        check_vma=False,
    )
```

```python
import jax
import jax.numpy as jnp
from jax import lax
from jax.experimental import pallas as pl
from jax.experimental.pallas import tpu as pltpu
from jax.sharding import Mesh
from jax.sharding import PartitionSpec as P

EPSILON = 1e-05
NY, NZ, NX, NC = 4, 8, 4, 2
BLOCKS = NY * NZ
PARTS = NX * NC
D = 8192
VOC = 128
PIECES = 8
SHARD = 2048
CAP = 32
FEAT = D // PARTS
WIDE = D // NZ
EXTRA = 128
TOK = 1024
HALF = WIDE // 2
MIB = 1 << 20
MOST = 56 * MIB
SHIFTS = (0, 1, 2, -1)

VMEM = pl.BlockSpec(memory_space=pltpu.VMEM)
SMEM = pl.BlockSpec(memory_space=pltpu.SMEM)
ANY = pl.BlockSpec(memory_space=pltpu.HBM)


def dot(left, right):
    return jnp.dot(left, right, preferred_element_type=jnp.float32)


def dot_dims(left, right, left_dim, right_dim):
    return lax.dot_general(
        left, right, (((left_dim,), (right_dim,)), ((), ())), preferred_element_type=jnp.float32
    )


def call(kernel, out_shape, in_specs, scratch=(), limit=16 * MIB):
    many = isinstance(out_shape, (tuple, list))
    return pl.pallas_call(
        kernel,
        out_shape=out_shape,
        in_specs=in_specs,
        out_specs=[VMEM] * len(out_shape) if many else VMEM,
        scratch_shapes=list(scratch),
        compiler_params=pltpu.CompilerParams(vmem_limit_bytes=limit),
    )


def shape(dims, kind):
    return jax.ShapeDtypeStruct(dims, kind)


def plan_kernel(pieces_ref, lengths_ref, request_ref, where_ref):
    row = lax.broadcasted_iota(jnp.int32, (VOC, VOC), 0)
    col = lax.broadcasted_iota(jnp.int32, (VOC, VOC), 1)
    earlier = (row < col).astype(jnp.float32).astype(jnp.bfloat16)
    level = lax.broadcasted_iota(jnp.int32, (BLOCKS, VOC), 0)
    lengths = lengths_ref[...]
    base = jnp.zeros((BLOCKS, 1), jnp.float32)
    high_sum = jnp.zeros((BLOCKS, CAP), jnp.float32)
    low_sum = jnp.zeros((BLOCKS, CAP), jnp.float32)
    for k in range(PIECES):
        piece = pieces_ref[k : k + 1, :]
        live = lengths > k
        block = jnp.where(live, piece >> 11, BLOCKS)
        local = piece & (SHARD - 1)
        onehot = (block == level).astype(jnp.float32)
        onehot16 = onehot.astype(jnp.bfloat16)
        before = dot(onehot16, earlier) + base
        rank = jnp.sum(before * onehot, axis=0, keepdims=True).astype(jnp.int32)
        base = base + jnp.sum(onehot, axis=1, keepdims=True)
        at_rank = rank == level
        high = jnp.where(at_rank, (local >> 6).astype(jnp.float32), 0.0).astype(jnp.bfloat16)
        low = jnp.where(at_rank, (local & 63).astype(jnp.float32), 0.0).astype(jnp.bfloat16)
        high_sum = high_sum + dot_dims(onehot16, high, 1, 1)
        low_sum = low_sum + dot_dims(onehot16, low, 1, 1)
        where_ref[k : k + 1, :] = jnp.where(live, block * CAP + rank, -1)
    request_ref[...] = high_sum.astype(jnp.int32) * 64 + low_sum.astype(jnp.int32)


def fetch_kernel(wanted_ref, table_ref, out_ref, onehot_buf, table_buf, sem):
    width = FEAT // 2
    copies = []
    for h in range(2):
        columns = pl.ds(h * width, width)
        copies.append(
            pltpu.make_async_copy(table_ref.at[:, columns], table_buf.at[:, columns], sem.at[h])
        )
        copies[h].start()
    eye = lax.broadcasted_iota(jnp.int32, (CAP, CAP), 0) == lax.broadcasted_iota(
        jnp.int32, (CAP, CAP), 1
    )
    lane = lax.broadcasted_iota(jnp.int32, (CAP, SHARD), 1)
    for g in range(BLOCKS):
        row = wanted_ref[g].astype(jnp.float32)
        column = jnp.sum(jnp.where(eye, row, 0.0), axis=1, keepdims=True).astype(jnp.int32)
        onehot_buf[g * CAP : (g + 1) * CAP, :] = (
            (lane == column).astype(jnp.float32).astype(jnp.bfloat16)
        )
    for h in range(2):
        copies[h].wait()
        columns = slice(h * width, (h + 1) * width)
        out_ref[:, columns] = dot(onehot_buf[...], table_buf[:, columns]).astype(jnp.bfloat16)


def embed_kernel(position_ref, table_ref, out_ref, onehot_buf):
    tile, count = 512, BLOCKS * VOC
    columns = jnp.concatenate(
        [position_ref[...], jnp.zeros((VOC - count // VOC, VOC), jnp.int32)], axis=0
    ).T
    lane = lax.broadcasted_iota(jnp.int32, (VOC, count), 1)
    for i in range(count // tile):
        for j in range(tile // VOC):
            n = i * (tile // VOC) + j
            onehot_buf[i % 2, j * VOC : (j + 1) * VOC, :] = (
                (lane == columns[:, n : n + 1]).astype(jnp.float32).astype(jnp.bfloat16)
            )
        rows = slice(i * tile, (i + 1) * tile)
        out_ref[rows, :] = dot(onehot_buf[i % 2], table_ref[...]).astype(jnp.bfloat16)


def spread_kernel(gain_ref, where_ref, out_ref):
    lane = lax.broadcasted_iota(jnp.int32, (VOC, BLOCKS * CAP), 1)
    columns = jnp.concatenate(
        [where_ref[...], jnp.zeros((VOC - PIECES, VOC), jnp.int32)], axis=0
    ).T
    total = jnp.zeros((VOC, BLOCKS * CAP), jnp.float32)
    for k in range(PIECES):
        total = jnp.where(columns[:, k : k + 1] == lane, gain_ref[k], total)
    for term in range(3):
        part = total.astype(jnp.bfloat16)
        out_ref[term] = part
        total = total - part.astype(jnp.float32)


def pool_kernel(spread_ref, rows_ref, gain_ref, out_ref):
    rows = rows_ref[...]
    pooled = dot(spread_ref[2], rows) + dot(spread_ref[1], rows) + dot(spread_ref[0], rows)
    out_ref[...] = (pooled * gain_ref[...]).astype(jnp.bfloat16)


def split_two(value, lane):
    high = value.astype(jnp.bfloat16)
    low = (value - high.astype(jnp.float32)).astype(jnp.bfloat16)
    return jnp.where(
        lane == 0, high.astype(jnp.float32), jnp.where(lane == 1, low.astype(jnp.float32), 0.0)
    ).astype(jnp.bfloat16)


def gather_rows(place_ref, refs, rows_buf):
    z = place_ref[0]
    for step, ref in zip((0, -1, 1, -2, 2, -3, 3), refs):
        at = lax.rem(z + (step + NZ), NZ)
        rows_buf[pl.ds(pl.multiple_of(at * VOC, VOC), VOC), :] = ref[...]
    at = lax.rem(z + 4, NZ)
    half = VOC // 2
    rows_buf[pl.ds(pl.multiple_of(at * VOC, half), half), :] = refs[7][...]
    rows_buf[pl.ds(pl.multiple_of(at * VOC + half, half), half), :] = refs[8][...]


def project_out_kernel(place_ref, order_ref, scale_ref, *refs):
    keep_ref, give_ref, rows_buf, result_buf, square_buf = refs[-5:]
    core = place_ref[1]
    gather_rows(place_ref, refs[:9], rows_buf)
    for q in range(NY):
        result_buf[order_ref[q]] = dot(rows_buf[...], refs[9][q])
    lane = lax.broadcasted_iota(jnp.int32, (VOC, EXTRA), 1)
    scale = scale_ref[...]
    for i in range(PARTS):
        wide = rows_buf[i * VOC : (i + 1) * VOC, :].astype(jnp.float32)
        square = jnp.sum(wide * wide * scale, axis=1, keepdims=True)
        square_buf[i] = split_two(square, lane)
    for i in range(NX):
        mine, other = 2 * i + core, 2 * i + 1 - core
        for q in range(NY):
            columns = slice(q * 256, (q + 1) * 256)
            keep_ref[i, :, columns] = result_buf[q, pl.ds(pl.multiple_of(mine * VOC, VOC), VOC), :]
            give_ref[i, :, columns] = result_buf[
                q, pl.ds(pl.multiple_of(other * VOC, VOC), VOC), :
            ].astype(jnp.bfloat16)
        keep_ref[i, :, WIDE:] = square_buf[mine].astype(jnp.float32)
        give_ref[i, :, WIDE:] = square_buf[other]


def project_in_kernel(place_ref, *refs):
    weight_ref, out_ref, rows_buf = refs[-3:]
    gather_rows(place_ref, refs[:9], rows_buf)
    for q in range(NY):
        out_ref[:, q * 256 : (q + 1) * 256] = dot(rows_buf[...], weight_ref[q])


def add_kernel(place_ref, keep_ref, got_ref, *out_refs):
    x = place_ref[3] >> 1
    lane = lax.broadcasted_iota(jnp.int32, (VOC, EXTRA), 1)
    for k, out_ref in zip(SHIFTS, out_refs):
        i = lax.rem(x + (k + NX), NX)
        total = keep_ref[i] + got_ref[i].astype(jnp.float32)
        out_ref[:, :WIDE] = total[:, :WIDE].astype(jnp.bfloat16)
        square = jnp.sum(total[:, WIDE:], axis=1, keepdims=True)
        out_ref[:, WIDE:] = split_two(square, lane)


def total_of(refs):
    total = refs[0][...].astype(jnp.float32)
    for ref in refs[1:]:
        total = total + ref[...].astype(jnp.float32)
    return total


def norm_kernel(*refs):
    first_ref, second_ref, inverse_ref = refs[NX:]
    total = total_of(refs[:NX])
    square = jnp.sum(total[:, WIDE:], axis=1, keepdims=True)
    inverse = lax.rsqrt(square / D + EPSILON)
    rows = total[:, :WIDE] * inverse
    first_ref[...] = rows[:, :HALF].T.astype(jnp.bfloat16)
    second_ref[...] = rows[:, HALF:].T.astype(jnp.bfloat16)
    inverse_ref[...] = inverse


def scale_kernel(place_ref, inverse_ref, total_ref, *out_refs):
    rows = (total_ref[...] * inverse_ref[...]).astype(jnp.bfloat16)
    for q in range(NY):
        for k, out_ref in zip(SHIFTS, out_refs):

            @pl.when(lax.rem(place_ref[2] + (k + NY), NY) == q)
            def _():
                out_ref[:VOC, :] = rows[:, q * 256 : q * 256 + VOC]
                out_ref[VOC:, :] = rows[:, q * 256 + VOC : (q + 1) * 256]


def shift_by(value, axis, step):
    count = {"y": NY, "z": NZ, "x": NX, "c": NC}[axis]
    return lax.ppermute(value, axis, [(i, (i + step) % count) for i in range(count)])


def z_ring(rows, first, beside):
    p1, m1 = shift_by(rows, "z", 1), shift_by(rows, "z", -1)
    p2, m2 = shift_by(p1, "z", 1), shift_by(m1, "z", -1)
    p2, m2, made = lax.optimization_barrier((p2, m2, beside(p1)))
    p3, m3 = shift_by(p2, "z", 1), shift_by(m2, "z", -1)
    p4, m4 = shift_by(p3[:first], "z", 1), shift_by(m3[first:], "z", -1)
    return [rows, p1, m1, p2, m2, p3, m3, p4, m4], made


def y_all(block):
    return [block] + [shift_by(block, "y", -step) for step in SHIFTS[1:]]


def deal(blocks, axis):
    return [blocks[0]] + [shift_by(b, axis, k) for b, k in zip(blocks[1:], SHIFTS[1:])]


def accumulate(shifts, routes, arrays, place_ref, hidden_ref, total_ref, bufs):
    hidden_buf, rows_buf, hidden_sem, rows_sem = bufs
    y, z = place_ref[2], place_ref[0]
    waits = [[] for _ in shifts]
    for slot, step in enumerate(shifts):
        at = lax.rem(z + (step + NZ), NZ)
        for q in range(NY):
            copy = pltpu.make_async_copy(
                hidden_ref.at[2 * q + at // 4, :, pl.ds(pl.multiple_of((at % 4) * 256, 256), 256)],
                hidden_buf.at[slot, :, pl.ds(q * 256, 256)],
                hidden_sem.at[slot, q],
            )
            copy.start()
            waits[slot].append(copy)
        for number, (index, from_row, rows, dy, dz, to_row) in enumerate(routes):
            if dz != step:
                continue
            at_y = lax.rem(y + (dy + NY), NY)
            copy = pltpu.make_async_copy(
                arrays[index].at[pl.ds(from_row, rows)],
                rows_buf.at[slot, pl.ds(to_row, rows), pl.ds(pl.multiple_of(at_y * VOC, VOC), VOC)],
                rows_sem.at[number],
            )
            copy.start()
            waits[slot].append(copy)
    tile = 256
    for slot in range(len(shifts)):
        for copy in waits[slot]:
            copy.wait()
        for i in range(TOK // tile):
            rows = pl.ds(i * tile, tile)
            product = dot(hidden_buf[slot, rows, :], rows_buf[slot])
            total_ref[rows, :] = total_ref[rows, :] + product


def near_kernel(shifts, routes, count, place_ref, hidden_ref, *refs):
    arrays, total_ref = refs[:count], refs[count]
    total_ref[...] = jnp.zeros_like(total_ref)
    accumulate(shifts, routes, arrays, place_ref, hidden_ref, total_ref, refs[count + 1 :])


def middle_kernel(shifts, routes, count, place_ref, total_in, hidden_ref, *refs):
    arrays, total_ref = refs[:count], refs[count]
    total_ref[...] = total_in[...]
    accumulate(shifts, routes, arrays, place_ref, hidden_ref, total_ref, refs[count + 1 :])


def far_kernel(shifts, routes, count, place_ref, target_ref, total_in, hidden_ref, *refs):
    arrays, out_ref, total_ref = refs[:count], refs[count], refs[count + 1]
    total_ref[...] = total_in[...]
    accumulate(shifts, routes, arrays, place_ref, hidden_ref, total_ref, refs[count + 2 :])
    part = place_ref[3]
    tile = 256
    column = lax.broadcasted_iota(jnp.int32, (tile, NY * VOC), 1)
    token_of = (column // VOC) * (NZ * VOC) + part * VOC + column % VOC
    lane = lax.broadcasted_iota(jnp.int32, (tile, 128), 1)
    for i in range(TOK // tile):
        rows = pl.ds(i * tile, tile)
        total = total_ref[rows, :]
        best = jnp.max(total, axis=1, keepdims=True)
        spread = jnp.sum(jnp.exp(total - best), axis=1, keepdims=True)
        hit = jnp.sum(jnp.where(token_of == target_ref[rows, :], total, 0.0), axis=1, keepdims=True)
        packed = jnp.where(lane == 0, best, jnp.where(lane == 1, spread, hit))
        turned = packed.T
        for j in range(tile // 128):
            out_ref[i * (tile // 128) + j] = turned[:8, j * 128 : (j + 1) * 128]


def merge_kernel(parts_ref, out_ref):
    best = parts_ref[0, 0:1, :]
    for i in range(1, PARTS):
        best = jnp.maximum(best, parts_ref[i, 0:1, :])
    spread = jnp.zeros_like(best)
    hit = jnp.zeros_like(best)
    for i in range(PARTS):
        spread = spread + parts_ref[i, 1:2, :] * jnp.exp(parts_ref[i, 0:1, :] - best)
        hit = hit + parts_ref[i, 2:3, :]
    out_ref[...] = best + jnp.log(spread) - hit


def swap(value, axes):
    return lax.all_to_all(value, axes, split_axis=0, concat_axis=0, tiled=True)


def after(value, *others):
    return lax.optimization_barrier((value, *others))[0]


def on_device(
    old_table, pieces, lengths, pos_gain, hyp_gain, w_in, w_out, hidden, token_ids, targets
):
    y, z = lax.axis_index("y"), lax.axis_index("z")
    core = lax.axis_index("c")
    part = lax.axis_index(("x", "c"))
    place = jnp.stack([z, core, y, part]).astype(jnp.int32)
    gain_row = hyp_gain.reshape(1, FEAT)
    target_column = targets.reshape(TOK, 1)

    hidden_all = lax.all_gather(hidden, ("x", "c"), axis=0)

    requests, where = call(
        plan_kernel,
        [shape((BLOCKS, CAP), jnp.int32), shape((PIECES, VOC), jnp.int32)],
        [VMEM, VMEM],
    )(pieces.T, lengths.reshape(1, VOC))
    wanted = swap(requests.reshape(BLOCKS, 1, CAP), ("y", "z"))
    found = call(
        fetch_kernel,
        shape((BLOCKS * CAP, FEAT), jnp.bfloat16),
        [VMEM, ANY],
        [
            pltpu.VMEM((BLOCKS * CAP, SHARD), jnp.bfloat16),
            pltpu.VMEM((SHARD, FEAT), jnp.bfloat16),
            pltpu.SemaphoreType.DMA((2,)),
        ],
        MOST,
    )(wanted, old_table)
    fetched = swap(found.reshape(BLOCKS, CAP, FEAT), ("y", "z"))
    spread = call(
        spread_kernel, shape((3, VOC, BLOCKS * CAP), jnp.bfloat16), [SMEM, VMEM]
    )(pos_gain, where)
    w_in_all = lax.all_gather(after(w_in, found), "y", axis=0)
    w_out_all = y_all(after(w_out, found))
    fetched, *w_out_all = lax.optimization_barrier((fetched, *w_out_all))
    pooled = call(pool_kernel, shape((VOC, FEAT), jnp.bfloat16), [VMEM, VMEM, VMEM])(
        spread, fetched.reshape(BLOCKS * CAP, FEAT), gain_row
    )

    group, w_out_all = z_ring(
        pooled, VOC // 2, lambda there: jnp.stack(lax.optimization_barrier((w_out_all, there))[0])
    )
    inverse_gain = 1.0 / (gain_row * gain_row)

    order = (y + jnp.array(SHIFTS, jnp.int32)) % NY
    w_out_all, hidden_all = lax.optimization_barrier((w_out_all, hidden_all))
    wider = WIDE + EXTRA
    keep, give = call(
        project_out_kernel,
        [shape((NX, VOC, wider), jnp.float32), shape((NX, VOC, wider), jnp.bfloat16)],
        [SMEM, SMEM] + [VMEM] * 11,
        [
            pltpu.VMEM((NZ * VOC, FEAT), jnp.bfloat16),
            pltpu.VMEM((NY, NZ * VOC, 256), jnp.float32),
            pltpu.VMEM((PARTS, VOC, EXTRA), jnp.bfloat16),
        ],
    )(place, order, inverse_gain, *group, w_out_all)
    chip_out = call(
        add_kernel, [shape((VOC, wider), jnp.bfloat16)] * NX, [SMEM, VMEM, VMEM]
    )(place, keep, shift_by(give, "c", 1))

    def tie(*values):
        return lax.optimization_barrier(values)

    chip_out, w_in_all = tie(chip_out, w_in_all)
    partial_in = call(
        project_in_kernel,
        shape((NZ * VOC, WIDE), jnp.float32),
        [SMEM] + [VMEM] * 10,
        [pltpu.VMEM((NZ * VOC, FEAT), jnp.bfloat16)],
    )(place, *group, w_in_all)
    out_parts, partial_in = tie(deal(chip_out, "x"), partial_in)
    total_in = lax.psum_scatter(partial_in, ("x", "c"), scatter_dimension=0, tiled=True)
    first_half, second_half, inverse = call(
        norm_kernel,
        [shape((HALF, VOC), jnp.bfloat16)] * 2 + [shape((VOC, 1), jnp.float32)],
        [VMEM] * NX,
    )(*out_parts)

    def step(pair):
        return [shift_by(pair[0], "z", 1), shift_by(pair[1], "z", -1)]

    first_half, second_half = tie(first_half, second_half)
    own_y, a1 = tie(y_all(second_half), step([first_half, first_half]))
    column = jnp.concatenate(own_y, axis=0)
    pair_1 = [jnp.concatenate([a, column], axis=0) for a in a1]
    stack_1 = jnp.concatenate([first_half, *a1], axis=0)

    pair_1, stack_1 = tie(pair_1, stack_1)
    ring_1, pair_2 = tie(y_all(stack_1), step(pair_1))

    pair_2, stack_2 = tie(pair_2, jnp.concatenate([m[:HALF] for m in pair_2], axis=0))
    ring_2, pair_3 = tie(y_all(stack_2), step(pair_2))

    input_rows = call(
        scale_kernel, [shape((256, VOC), jnp.bfloat16)] * NY, [SMEM, VMEM, VMEM]
    )(place, inverse, total_in)
    stack_3 = [m[:HALF] for m in pair_3]
    stacks = [jnp.concatenate([*stack_3, chunk], axis=0) for chunk in input_rows]
    pair_3, stacks = tie(pair_3, stacks)
    def take(kind, array, entries):
        for entry in entries:
            kind[1].append((len(kind[0]), *entry))
        kind[0].append(array)

    def column_at(low, dz):
        return [(low + i * HALF, HALF, dy, dz, HALF) for i, dy in enumerate(SHIFTS)]

    def others(shifts, arrays):
        return list(zip(shifts, arrays))[1:]

    def buffers(shifts, routes):
        return [
            pltpu.VMEM((len(shifts), TOK, WIDE), jnp.bfloat16),
            pltpu.VMEM((len(shifts), WIDE, NY * VOC), jnp.bfloat16),
            pltpu.SemaphoreType.DMA((len(shifts), NY)),
            pltpu.SemaphoreType.DMA((len(routes),)),
        ]

    near, middle, far = ([], []), ([], []), ([], [])
    take(near, column, column_at(0, 0))
    take(near, first_half, [(0, HALF, 0, 0, 0)])
    for a, dz in zip(a1, (-1, 1)):
        take(near, a, [(0, HALF, 0, dz, 0)])
    for m, dz in zip(pair_2, (-1, 1)):
        take(near, m, [(0, HALF, 0, 2 * dz, 0), *column_at(HALF, dz)])
    for m, dz in zip(pair_3, (-1, 1)):
        take(near, m, column_at(HALF, 2 * dz))
    for dy, array in others(SHIFTS, ring_1):
        take(near, array, [(i * HALF, HALF, dy, dz, 0) for i, dz in enumerate((0, -1, 1))])
    for dy, array in others(SHIFTS, ring_2):
        take(near, array, [(i * HALF, HALF, dy, dz, 0) for i, dz in enumerate((-2, 2))])

    logits_shape = shape((TOK, NY * VOC), jnp.float32)
    near_shifts, middle_shifts, far_shifts = (0, -1, 1, -2, 2), (-3, 3), (4,)
    total = call(
        lambda *refs: near_kernel(near_shifts, near[1], len(near[0]), *refs),
        logits_shape,
        [SMEM, ANY] + [ANY] * len(near[0]),
        buffers(near_shifts, near[1]),
        MOST,
    )(place, hidden_all, *near[0])
    ring_3, pair_4, total = tie(deal(stacks, "y"), step(pair_3), total)
    chunks = [array[2 * HALF :] for array in ring_3]
    chunks = [jnp.concatenate([c[:VOC], c[VOC:]], axis=1) for c in chunks]
    in_table = lax.all_gather(jnp.concatenate(chunks, axis=0), ("x", "c"), axis=0)

    for m, dz in zip(pair_3, (-1, 1)):
        take(middle, m, [(0, HALF, 0, 3 * dz, 0)])
    for m, dz in zip(pair_4, (-1, 1)):
        take(middle, m, column_at(HALF, 3 * dz))
    for dy, array in others([-k for k in SHIFTS], ring_3):
        take(middle, array, [(i * HALF, HALF, dy, dz, 0) for i, dz in enumerate((-3, 3))])
    last_a, last_b = pair_4[1][:HALF], [pair_4[0][HALF : 3 * HALF], pair_4[1][3 * HALF :]]
    take(far, last_a, [(0, HALF, 0, 4, 0)])
    last_a, last_b, total = tie(last_a, last_b, total)
    total = call(
        lambda *refs: middle_kernel(middle_shifts, middle[1], len(middle[0]), *refs),
        logits_shape,
        [SMEM, VMEM, ANY] + [ANY] * len(middle[0]),
        buffers(middle_shifts, middle[1]),
        MOST,
    )(place, total, hidden_all, *middle[0])
    last_y, last_z, total = tie(y_all(last_a), step(last_b), total)
    for dy, array in others(SHIFTS, last_y):
        take(far, array, [(0, HALF, dy, 4, 0)])
    for half, array in enumerate(last_z):
        dys = SHIFTS[2 * half : 2 * half + 2]
        take(far, array, [(i * HALF, HALF, dy, 4, HALF) for i, dy in enumerate(dys)])

    back = (y - (token_ids >> 10)) & 3
    position = ((token_ids >> 7) & 7) * (NY * VOC) + back * VOC + (token_ids & 127)
    embedded = call(
        embed_kernel,
        shape((BLOCKS * VOC, 256), jnp.bfloat16),
        [VMEM, VMEM],
        [pltpu.VMEM((2, 512, BLOCKS * VOC), jnp.bfloat16)],
        20 * MIB,
    )(position.reshape(-1, VOC), in_table.reshape(BLOCKS * VOC, 256))

    stats = call(
        lambda *refs: far_kernel(far_shifts, far[1], len(far[0]), *refs),
        shape((PARTS, 8, 128), jnp.float32),
        [SMEM, VMEM, VMEM, ANY] + [ANY] * len(far[0]),
        [pltpu.VMEM((TOK, NY * VOC), jnp.float32), *buffers(far_shifts, far[1])],
        MOST,
    )(place, target_column, total, hidden_all, *far[0])
    merged, embedded = tie(swap(stats, ("x", "c")), embedded)
    loss = call(merge_kernel, shape((1, 128), jnp.float32), [VMEM])(merged)
    return (embedded, loss.reshape(128))


def solution(mesh):
    grid = Mesh(mesh.devices.reshape(NY, NZ, NX, NC), ("y", "z", "x", "c"))
    vocab, seq = ("y", "z"), ("x", "c")
    return jax.shard_map(
        on_device,
        mesh=grid,
        in_specs=(
            P(vocab, seq),
            P(vocab, None),
            P(vocab),
            P(),
            P(seq),
            P(seq, vocab),
            P(seq, vocab),
            P(vocab, seq),
            P(seq),
            P(vocab),
        ),
        out_specs=(P(seq, vocab), P((*vocab, *seq))),
        check_vma=False,
    )
```

```python
import jax
import jax.numpy as jnp
from jax import lax
from jax.experimental import pallas as pl
from jax.experimental.pallas import tpu as pltpu
from jax.sharding import Mesh
from jax.sharding import PartitionSpec as P

EPSILON = 1e-05
NY, NZ, NX, NC = 4, 8, 4, 2
BLOCKS = NY * NZ
PARTS = NX * NC
D = 8192
VOC = 128
PIECES = 8
SHARD = 2048
CAP = 32
FEAT = D // PARTS
WIDE = D // NZ
EXTRA = 128
TOK = 1024
HALF = WIDE // 2
MIB = 1 << 20
MOST = 56 * MIB
SHIFTS = (0, 1, -1, 2)

VMEM = pl.BlockSpec(memory_space=pltpu.VMEM)
SMEM = pl.BlockSpec(memory_space=pltpu.SMEM)
ANY = pl.BlockSpec(memory_space=pltpu.HBM)


def dot(left, right):
    return jnp.dot(left, right, preferred_element_type=jnp.float32)


def dot_dims(left, right, left_dim, right_dim):
    return lax.dot_general(
        left, right, (((left_dim,), (right_dim,)), ((), ())), preferred_element_type=jnp.float32
    )


def call(kernel, out_shape, in_specs, scratch=(), limit=16 * MIB):
    many = isinstance(out_shape, (tuple, list))
    return pl.pallas_call(
        kernel,
        out_shape=out_shape,
        in_specs=in_specs,
        out_specs=[VMEM] * len(out_shape) if many else VMEM,
        scratch_shapes=list(scratch),
        compiler_params=pltpu.CompilerParams(vmem_limit_bytes=limit),
    )


def shape(dims, kind):
    return jax.ShapeDtypeStruct(dims, kind)


def plan_kernel(pieces_ref, lengths_ref, request_ref, where_ref):
    row = lax.broadcasted_iota(jnp.int32, (VOC, VOC), 0)
    col = lax.broadcasted_iota(jnp.int32, (VOC, VOC), 1)
    earlier = (row < col).astype(jnp.float32).astype(jnp.bfloat16)
    level = lax.broadcasted_iota(jnp.int32, (BLOCKS, VOC), 0)
    lengths = lengths_ref[...]
    base = jnp.zeros((BLOCKS, 1), jnp.float32)
    high_sum = jnp.zeros((BLOCKS, CAP), jnp.float32)
    low_sum = jnp.zeros((BLOCKS, CAP), jnp.float32)
    for k in range(PIECES):
        piece = pieces_ref[k : k + 1, :]
        live = lengths > k
        block = jnp.where(live, piece >> 11, BLOCKS)
        local = piece & (SHARD - 1)
        onehot = (block == level).astype(jnp.float32)
        onehot16 = onehot.astype(jnp.bfloat16)
        before = dot(onehot16, earlier) + base
        rank = jnp.sum(before * onehot, axis=0, keepdims=True).astype(jnp.int32)
        base = base + jnp.sum(onehot, axis=1, keepdims=True)
        at_rank = rank == level
        high = jnp.where(at_rank, (local >> 6).astype(jnp.float32), 0.0).astype(jnp.bfloat16)
        low = jnp.where(at_rank, (local & 63).astype(jnp.float32), 0.0).astype(jnp.bfloat16)
        high_sum = high_sum + dot_dims(onehot16, high, 1, 1)
        low_sum = low_sum + dot_dims(onehot16, low, 1, 1)
        where_ref[k : k + 1, :] = jnp.where(live, block * CAP + rank, -1)
    request_ref[...] = high_sum.astype(jnp.int32) * 64 + low_sum.astype(jnp.int32)


def fetch_kernel(wanted_ref, table_ref, out_ref, onehot_buf, table_buf, sem):
    width = FEAT // 2
    copies = []
    for h in range(2):
        columns = pl.ds(h * width, width)
        copies.append(
            pltpu.make_async_copy(table_ref.at[:, columns], table_buf.at[:, columns], sem.at[h])
        )
        copies[h].start()
    eye = lax.broadcasted_iota(jnp.int32, (CAP, CAP), 0) == lax.broadcasted_iota(
        jnp.int32, (CAP, CAP), 1
    )
    lane = lax.broadcasted_iota(jnp.int32, (CAP, SHARD), 1)
    for g in range(BLOCKS):
        row = wanted_ref[g].astype(jnp.float32)
        column = jnp.sum(jnp.where(eye, row, 0.0), axis=1, keepdims=True).astype(jnp.int32)
        onehot_buf[g * CAP : (g + 1) * CAP, :] = (
            (lane == column).astype(jnp.float32).astype(jnp.bfloat16)
        )
    for h in range(2):
        copies[h].wait()
        columns = slice(h * width, (h + 1) * width)
        out_ref[:, columns] = dot(onehot_buf[...], table_buf[:, columns]).astype(jnp.bfloat16)


def embed_kernel(position_ref, table_ref, out_ref, onehot_buf):
    tile, count = 512, BLOCKS * VOC
    columns = jnp.concatenate(
        [position_ref[...], jnp.zeros((VOC - count // VOC, VOC), jnp.int32)], axis=0
    ).T
    lane = lax.broadcasted_iota(jnp.int32, (VOC, count), 1)
    for i in range(count // tile):
        for j in range(tile // VOC):
            n = i * (tile // VOC) + j
            onehot_buf[i % 2, j * VOC : (j + 1) * VOC, :] = (
                (lane == columns[:, n : n + 1]).astype(jnp.float32).astype(jnp.bfloat16)
            )
        rows = slice(i * tile, (i + 1) * tile)
        out_ref[rows, :] = dot(onehot_buf[i % 2], table_ref[...]).astype(jnp.bfloat16)


def spread_kernel(gain_ref, where_ref, out_ref):
    lane = lax.broadcasted_iota(jnp.int32, (VOC, BLOCKS * CAP), 1)
    columns = jnp.concatenate(
        [where_ref[...], jnp.zeros((VOC - PIECES, VOC), jnp.int32)], axis=0
    ).T
    total = jnp.zeros((VOC, BLOCKS * CAP), jnp.float32)
    for k in range(PIECES):
        total = jnp.where(columns[:, k : k + 1] == lane, gain_ref[k], total)
    for term in range(3):
        part = total.astype(jnp.bfloat16)
        out_ref[term] = part
        total = total - part.astype(jnp.float32)


def pool_kernel(spread_ref, rows_ref, gain_ref, out_ref):
    rows = rows_ref[...]
    pooled = dot(spread_ref[2], rows) + dot(spread_ref[1], rows) + dot(spread_ref[0], rows)
    out_ref[...] = (pooled * gain_ref[...]).astype(jnp.bfloat16)


def split_two(value, lane):
    high = value.astype(jnp.bfloat16)
    low = (value - high.astype(jnp.float32)).astype(jnp.bfloat16)
    return jnp.where(
        lane == 0, high.astype(jnp.float32), jnp.where(lane == 1, low.astype(jnp.float32), 0.0)
    ).astype(jnp.bfloat16)


def gather_rows(place_ref, refs, rows_buf):
    z = place_ref[0]
    for step, ref in zip((0, -1, 1, -2, 2, -3, 3), refs):
        at = lax.rem(z + (step + NZ), NZ)
        rows_buf[pl.ds(pl.multiple_of(at * VOC, VOC), VOC), :] = ref[...]
    at = lax.rem(z + 4, NZ)
    half = VOC // 2
    rows_buf[pl.ds(pl.multiple_of(at * VOC, half), half), :] = refs[7][...]
    rows_buf[pl.ds(pl.multiple_of(at * VOC + half, half), half), :] = refs[8][...]


def project_out_kernel(place_ref, order_ref, scale_ref, *refs):
    keep_ref, give_ref, rows_buf, result_buf, square_buf = refs[-5:]
    core = place_ref[1]
    gather_rows(place_ref, refs[:9], rows_buf)
    for q in range(NY):
        result_buf[order_ref[q]] = dot(rows_buf[...], refs[9][q])
    lane = lax.broadcasted_iota(jnp.int32, (VOC, EXTRA), 1)
    scale = scale_ref[...]
    for i in range(PARTS):
        wide = rows_buf[i * VOC : (i + 1) * VOC, :].astype(jnp.float32)
        square = jnp.sum(wide * wide * scale, axis=1, keepdims=True)
        square_buf[i] = split_two(square, lane)
    for i in range(NX):
        mine, other = 2 * i + core, 2 * i + 1 - core
        for q in range(NY):
            columns = slice(q * 256, (q + 1) * 256)
            keep_ref[i, :, columns] = result_buf[q, pl.ds(pl.multiple_of(mine * VOC, VOC), VOC), :]
            give_ref[i, :, columns] = result_buf[
                q, pl.ds(pl.multiple_of(other * VOC, VOC), VOC), :
            ].astype(jnp.bfloat16)
        keep_ref[i, :, WIDE:] = square_buf[mine].astype(jnp.float32)
        give_ref[i, :, WIDE:] = square_buf[other]


def project_in_kernel(place_ref, *refs):
    weight_ref, out_ref, rows_buf = refs[-3:]
    gather_rows(place_ref, refs[:9], rows_buf)
    for q in range(NY):
        out_ref[:, q * 256 : (q + 1) * 256] = dot(rows_buf[...], weight_ref[q])


def add_kernel(place_ref, keep_ref, got_ref, *out_refs):
    x = place_ref[3] >> 1
    lane = lax.broadcasted_iota(jnp.int32, (VOC, EXTRA), 1)
    for k, out_ref in zip(SHIFTS, out_refs):
        i = lax.rem(x + (k + NX), NX)
        total = keep_ref[i] + got_ref[i].astype(jnp.float32)
        out_ref[:, :WIDE] = total[:, :WIDE].astype(jnp.bfloat16)
        square = jnp.sum(total[:, WIDE:], axis=1, keepdims=True)
        out_ref[:, WIDE:] = split_two(square, lane)


def total_of(refs):
    total = refs[0][...].astype(jnp.float32)
    for ref in refs[1:]:
        total = total + ref[...].astype(jnp.float32)
    return total


def norm_kernel(*refs):
    first_ref, second_ref, inverse_ref = refs[NX:]
    total = total_of(refs[:NX])
    square = jnp.sum(total[:, WIDE:], axis=1, keepdims=True)
    inverse = lax.rsqrt(square / D + EPSILON)
    rows = total[:, :WIDE] * inverse
    first_ref[...] = rows[:, :HALF].T.astype(jnp.bfloat16)
    second_ref[...] = rows[:, HALF:].T.astype(jnp.bfloat16)
    inverse_ref[...] = inverse


def scale_kernel(place_ref, inverse_ref, total_ref, *out_refs):
    rows = (total_ref[...] * inverse_ref[...]).astype(jnp.bfloat16)
    for q in range(NY):
        for k, out_ref in zip(SHIFTS, out_refs):

            @pl.when(lax.rem(place_ref[2] + (k + NY), NY) == q)
            def _():
                out_ref[:VOC, :] = rows[:, q * 256 : q * 256 + VOC]
                out_ref[VOC:, :] = rows[:, q * 256 + VOC : (q + 1) * 256]


def shift_by(value, axis, step):
    count = {"y": NY, "z": NZ, "x": NX, "c": NC}[axis]
    return lax.ppermute(value, axis, [(i, (i + step) % count) for i in range(count)])


def z_ring(rows, first, beside):
    p1, m1 = shift_by(rows, "z", 1), shift_by(rows, "z", -1)
    p2, m2 = shift_by(p1, "z", 1), shift_by(m1, "z", -1)
    p2, m2, made = lax.optimization_barrier((p2, m2, beside(p1)))
    p3, m3 = shift_by(p2, "z", 1), shift_by(m2, "z", -1)
    p4, m4 = shift_by(p3[:first], "z", 1), shift_by(m3[first:], "z", -1)
    return [rows, p1, m1, p2, m2, p3, m3, p4, m4], made


def y_all(block):
    return [block] + [shift_by(block, "y", -step) for step in SHIFTS[1:]]


def deal(blocks, axis):
    return [blocks[0]] + [shift_by(b, axis, k) for b, k in zip(blocks[1:], SHIFTS[1:])]


def accumulate(shifts, routes, arrays, place_ref, hidden_ref, total_ref, bufs):
    hidden_buf, rows_buf, hidden_sem, rows_sem = bufs
    y, z = place_ref[2], place_ref[0]
    waits = [[] for _ in shifts]
    for slot, step in enumerate(shifts):
        at = lax.rem(z + (step + NZ), NZ)
        for q in range(NY):
            copy = pltpu.make_async_copy(
                hidden_ref.at[2 * q + at // 4, :, pl.ds(pl.multiple_of((at % 4) * 256, 256), 256)],
                hidden_buf.at[slot, :, pl.ds(q * 256, 256)],
                hidden_sem.at[slot, q],
            )
            copy.start()
            waits[slot].append(copy)
        for number, (index, from_row, rows, dy, dz, to_row) in enumerate(routes):
            if dz != step:
                continue
            at_y = lax.rem(y + (dy + NY), NY)
            copy = pltpu.make_async_copy(
                arrays[index].at[pl.ds(from_row, rows)],
                rows_buf.at[slot, pl.ds(to_row, rows), pl.ds(pl.multiple_of(at_y * VOC, VOC), VOC)],
                rows_sem.at[number],
            )
            copy.start()
            waits[slot].append(copy)
    tile = 256
    for slot in range(len(shifts)):
        for copy in waits[slot]:
            copy.wait()
        for i in range(TOK // tile):
            rows = pl.ds(i * tile, tile)
            product = dot(hidden_buf[slot, rows, :], rows_buf[slot])
            total_ref[rows, :] = total_ref[rows, :] + product


def near_kernel(shifts, routes, count, place_ref, hidden_ref, *refs):
    arrays, total_ref = refs[:count], refs[count]
    total_ref[...] = jnp.zeros_like(total_ref)
    accumulate(shifts, routes, arrays, place_ref, hidden_ref, total_ref, refs[count + 1 :])


def middle_kernel(shifts, routes, count, place_ref, total_in, hidden_ref, *refs):
    arrays, total_ref = refs[:count], refs[count]
    total_ref[...] = total_in[...]
    accumulate(shifts, routes, arrays, place_ref, hidden_ref, total_ref, refs[count + 1 :])


def far_kernel(shifts, routes, count, place_ref, target_ref, total_in, hidden_ref, *refs):
    arrays, out_ref, total_ref = refs[:count], refs[count], refs[count + 1]
    total_ref[...] = total_in[...]
    accumulate(shifts, routes, arrays, place_ref, hidden_ref, total_ref, refs[count + 2 :])
    part = place_ref[3]
    tile = 256
    column = lax.broadcasted_iota(jnp.int32, (tile, NY * VOC), 1)
    token_of = (column // VOC) * (NZ * VOC) + part * VOC + column % VOC
    lane = lax.broadcasted_iota(jnp.int32, (tile, 128), 1)
    for i in range(TOK // tile):
        rows = pl.ds(i * tile, tile)
        total = total_ref[rows, :]
        best = jnp.max(total, axis=1, keepdims=True)
        spread = jnp.sum(jnp.exp(total - best), axis=1, keepdims=True)
        hit = jnp.sum(jnp.where(token_of == target_ref[rows, :], total, 0.0), axis=1, keepdims=True)
        packed = jnp.where(lane == 0, best, jnp.where(lane == 1, spread, hit))
        turned = packed.T
        for j in range(tile // 128):
            out_ref[i * (tile // 128) + j] = turned[:8, j * 128 : (j + 1) * 128]


def merge_kernel(parts_ref, out_ref):
    best = parts_ref[0, 0:1, :]
    for i in range(1, PARTS):
        best = jnp.maximum(best, parts_ref[i, 0:1, :])
    spread = jnp.zeros_like(best)
    hit = jnp.zeros_like(best)
    for i in range(PARTS):
        spread = spread + parts_ref[i, 1:2, :] * jnp.exp(parts_ref[i, 0:1, :] - best)
        hit = hit + parts_ref[i, 2:3, :]
    out_ref[...] = best + jnp.log(spread) - hit


def swap(value, axes):
    return lax.all_to_all(value, axes, split_axis=0, concat_axis=0, tiled=True)


def after(value, *others):
    return lax.optimization_barrier((value, *others))[0]


def on_device(
    old_table, pieces, lengths, pos_gain, hyp_gain, w_in, w_out, hidden, token_ids, targets
):
    y, z = lax.axis_index("y"), lax.axis_index("z")
    core = lax.axis_index("c")
    part = lax.axis_index(("x", "c"))
    place = jnp.stack([z, core, y, part]).astype(jnp.int32)
    gain_row = hyp_gain.reshape(1, FEAT)
    target_column = targets.reshape(TOK, 1)

    hidden_all = lax.all_gather(hidden, ("x", "c"), axis=0)

    requests, where = call(
        plan_kernel,
        [shape((BLOCKS, CAP), jnp.int32), shape((PIECES, VOC), jnp.int32)],
        [VMEM, VMEM],
    )(pieces.T, lengths.reshape(1, VOC))
    wanted = swap(requests.reshape(BLOCKS, 1, CAP), ("y", "z"))
    found = call(
        fetch_kernel,
        shape((BLOCKS * CAP, FEAT), jnp.bfloat16),
        [VMEM, ANY],
        [
            pltpu.VMEM((BLOCKS * CAP, SHARD), jnp.bfloat16),
            pltpu.VMEM((SHARD, FEAT), jnp.bfloat16),
            pltpu.SemaphoreType.DMA((2,)),
        ],
        MOST,
    )(wanted, old_table)
    found, target_column = lax.optimization_barrier((found, target_column))
    fetched = swap(found.reshape(BLOCKS, CAP, FEAT), ("y", "z"))
    spread = call(
        spread_kernel, shape((3, VOC, BLOCKS * CAP), jnp.bfloat16), [SMEM, VMEM]
    )(pos_gain, where)
    w_in_all = lax.all_gather(after(w_in, found), "y", axis=0)
    w_out_all = y_all(after(w_out, found))
    fetched, *w_out_all = lax.optimization_barrier((fetched, *w_out_all))
    pooled = call(pool_kernel, shape((VOC, FEAT), jnp.bfloat16), [VMEM, VMEM, VMEM])(
        spread, fetched.reshape(BLOCKS * CAP, FEAT), gain_row
    )

    group, w_out_all = z_ring(
        pooled, VOC // 2, lambda there: jnp.stack(lax.optimization_barrier((w_out_all, there))[0])
    )
    inverse_gain = 1.0 / (gain_row * gain_row)

    order = (y + jnp.array(SHIFTS, jnp.int32)) % NY
    w_out_all, hidden_all = lax.optimization_barrier((w_out_all, hidden_all))
    wider = WIDE + EXTRA
    keep, give = call(
        project_out_kernel,
        [shape((NX, VOC, wider), jnp.float32), shape((NX, VOC, wider), jnp.bfloat16)],
        [SMEM, SMEM] + [VMEM] * 11,
        [
            pltpu.VMEM((NZ * VOC, FEAT), jnp.bfloat16),
            pltpu.VMEM((NY, NZ * VOC, 256), jnp.float32),
            pltpu.VMEM((PARTS, VOC, EXTRA), jnp.bfloat16),
        ],
    )(place, order, inverse_gain, *group, w_out_all)
    chip_out = call(
        add_kernel, [shape((VOC, wider), jnp.bfloat16)] * NX, [SMEM, VMEM, VMEM]
    )(place, keep, shift_by(give, "c", 1))

    def tie(*values):
        return lax.optimization_barrier(values)

    chip_out, w_in_all = tie(chip_out, w_in_all)
    partial_in = call(
        project_in_kernel,
        shape((NZ * VOC, WIDE), jnp.float32),
        [SMEM] + [VMEM] * 10,
        [pltpu.VMEM((NZ * VOC, FEAT), jnp.bfloat16)],
    )(place, *group, w_in_all)
    out_parts, partial_in = tie(deal(chip_out, "x"), partial_in)
    total_in = lax.psum_scatter(partial_in, ("x", "c"), scatter_dimension=0, tiled=True)
    first_half, second_half, inverse = call(
        norm_kernel,
        [shape((HALF, VOC), jnp.bfloat16)] * 2 + [shape((VOC, 1), jnp.float32)],
        [VMEM] * NX,
    )(*out_parts)

    def step(pair):
        return [shift_by(pair[0], "z", 1), shift_by(pair[1], "z", -1)]

    first_half, second_half = tie(first_half, second_half)
    own_y, a1 = tie(y_all(second_half), step([first_half, first_half]))
    column = jnp.concatenate(own_y, axis=0)
    pair_1 = [jnp.concatenate([a, column], axis=0) for a in a1]
    stack_1 = jnp.concatenate([first_half, *a1], axis=0)

    pair_1, stack_1 = tie(pair_1, stack_1)
    ring_1, pair_2 = tie(y_all(stack_1), step(pair_1))

    pair_2, stack_2 = tie(pair_2, jnp.concatenate([m[:HALF] for m in pair_2], axis=0))
    input_rows = call(
        scale_kernel, [shape((256, VOC), jnp.bfloat16)] * NY, [SMEM, VMEM, VMEM]
    )(place, inverse, total_in)
    ring_2, pair_3, input_rows = tie(y_all(stack_2), step(pair_2), input_rows)

    stack_3 = [m[:HALF] for m in pair_3]
    stacks = [jnp.concatenate([*stack_3, chunk], axis=0) for chunk in input_rows]
    pair_3, stacks = tie(pair_3, stacks)
    def take(kind, array, entries):
        for entry in entries:
            kind[1].append((len(kind[0]), *entry))
        kind[0].append(array)

    def column_at(low, dz):
        return [(low + i * HALF, HALF, dy, dz, HALF) for i, dy in enumerate(SHIFTS)]

    def others(shifts, arrays):
        return list(zip(shifts, arrays))[1:]

    def buffers(shifts, routes):
        return [
            pltpu.VMEM((len(shifts), TOK, WIDE), jnp.bfloat16),
            pltpu.VMEM((len(shifts), WIDE, NY * VOC), jnp.bfloat16),
            pltpu.SemaphoreType.DMA((len(shifts), NY)),
            pltpu.SemaphoreType.DMA((len(routes),)),
        ]

    near, middle, far = ([], []), ([], []), ([], [])
    take(near, column, column_at(0, 0))
    take(near, first_half, [(0, HALF, 0, 0, 0)])
    for a, dz in zip(a1, (-1, 1)):
        take(near, a, [(0, HALF, 0, dz, 0)])
    for m, dz in zip(pair_2, (-1, 1)):
        take(near, m, [(0, HALF, 0, 2 * dz, 0), *column_at(HALF, dz)])
    for m, dz in zip(pair_3, (-1, 1)):
        take(near, m, column_at(HALF, 2 * dz))
    for dy, array in others(SHIFTS, ring_1):
        take(near, array, [(i * HALF, HALF, dy, dz, 0) for i, dz in enumerate((0, -1, 1))])
    for dy, array in others(SHIFTS, ring_2):
        take(near, array, [(i * HALF, HALF, dy, dz, 0) for i, dz in enumerate((-2, 2))])

    logits_shape = shape((TOK, NY * VOC), jnp.float32)
    near_shifts, middle_shifts, far_shifts = (0, -1, 1, -2, 2), (-3, 3), (4,)
    total = call(
        lambda *refs: near_kernel(near_shifts, near[1], len(near[0]), *refs),
        logits_shape,
        [SMEM, ANY] + [ANY] * len(near[0]),
        buffers(near_shifts, near[1]),
        MOST,
    )(place, hidden_all, *near[0])
    ring_3, pair_4, total = tie(deal(stacks, "y"), step(pair_3), total)
    chunks = [array[2 * HALF :] for array in ring_3]
    chunks = [jnp.concatenate([c[:VOC], c[VOC:]], axis=1) for c in chunks]
    in_table = lax.all_gather(jnp.concatenate(chunks, axis=0), ("x", "c"), axis=0)

    for m, dz in zip(pair_3, (-1, 1)):
        take(middle, m, [(0, HALF, 0, 3 * dz, 0)])
    for m, dz in zip(pair_4, (-1, 1)):
        take(middle, m, column_at(HALF, 3 * dz))
    for dy, array in others([-k for k in SHIFTS], ring_3):
        take(middle, array, [(i * HALF, HALF, dy, dz, 0) for i, dz in enumerate((-3, 3))])
    last_a, last_b = pair_4[1][:HALF], [pair_4[0][HALF : 3 * HALF], pair_4[1][3 * HALF :]]
    take(far, last_a, [(0, HALF, 0, 4, 0)])
    last_a, last_b, total = tie(last_a, last_b, total)
    total = call(
        lambda *refs: middle_kernel(middle_shifts, middle[1], len(middle[0]), *refs),
        logits_shape,
        [SMEM, VMEM, ANY] + [ANY] * len(middle[0]),
        buffers(middle_shifts, middle[1]),
        MOST,
    )(place, total, hidden_all, *middle[0])
    last_y, last_z, total = tie(y_all(last_a), step(last_b), total)
    for dy, array in others(SHIFTS, last_y):
        take(far, array, [(0, HALF, dy, 4, 0)])
    for half, array in enumerate(last_z):
        dys = SHIFTS[2 * half : 2 * half + 2]
        take(far, array, [(i * HALF, HALF, dy, 4, HALF) for i, dy in enumerate(dys)])

    back = (y - (token_ids >> 10)) & 3
    back = back ^ (back >> 1)
    position = ((token_ids >> 7) & 7) * (NY * VOC) + back * VOC + (token_ids & 127)
    embedded = call(
        embed_kernel,
        shape((BLOCKS * VOC, 256), jnp.bfloat16),
        [VMEM, VMEM],
        [pltpu.VMEM((2, 512, BLOCKS * VOC), jnp.bfloat16)],
        20 * MIB,
    )(position.reshape(-1, VOC), in_table.reshape(BLOCKS * VOC, 256))

    stats = call(
        lambda *refs: far_kernel(far_shifts, far[1], len(far[0]), *refs),
        shape((PARTS, 8, 128), jnp.float32),
        [SMEM, VMEM, VMEM, ANY] + [ANY] * len(far[0]),
        [pltpu.VMEM((TOK, NY * VOC), jnp.float32), *buffers(far_shifts, far[1])],
        MOST,
    )(place, target_column, total, hidden_all, *far[0])
    merged, embedded = tie(swap(stats, ("x", "c")), embedded)
    loss = call(merge_kernel, shape((1, 128), jnp.float32), [VMEM])(merged)
    return (embedded, loss.reshape(128))


def solution(mesh):
    grid = Mesh(mesh.devices.reshape(NY, NZ, NX, NC), ("y", "z", "x", "c"))
    vocab, seq = ("y", "z"), ("x", "c")
    return jax.shard_map(
        on_device,
        mesh=grid,
        in_specs=(
            P(vocab, seq),
            P(vocab, None),
            P(vocab),
            P(),
            P(seq),
            P(seq, vocab),
            P(seq, vocab),
            P(vocab, seq),
            P(seq),
            P(vocab),
        ),
        out_specs=(P(seq, vocab), P((*vocab, *seq))),
        check_vma=False,
    )
```

```python
import jax
import jax.numpy as jnp
from jax import lax
from jax.experimental import pallas as pl
from jax.experimental.pallas import tpu as pltpu
from jax.sharding import Mesh
from jax.sharding import PartitionSpec as P

EPSILON = 1e-05
NY, NZ, NX, NC = 4, 8, 4, 2
BLOCKS = NY * NZ
PARTS = NX * NC
D = 8192
VOC = 128
PIECES = 8
SHARD = 2048
CAP = 32
FEAT = D // PARTS
WIDE = D // NZ
EXTRA = 128
TOK = 1024
HALF = WIDE // 2
MIB = 1 << 20
MOST = 56 * MIB
SHIFTS = (0, 1, -1, 2)

VMEM = pl.BlockSpec(memory_space=pltpu.VMEM)
SMEM = pl.BlockSpec(memory_space=pltpu.SMEM)
ANY = pl.BlockSpec(memory_space=pltpu.HBM)


def dot(left, right):
    return jnp.dot(left, right, preferred_element_type=jnp.float32)


def dot_dims(left, right, left_dim, right_dim):
    return lax.dot_general(
        left, right, (((left_dim,), (right_dim,)), ((), ())), preferred_element_type=jnp.float32
    )


def call(kernel, out_shape, in_specs, scratch=(), limit=16 * MIB, out_space=VMEM):
    many = isinstance(out_shape, (tuple, list))
    return pl.pallas_call(
        kernel,
        out_shape=out_shape,
        in_specs=in_specs,
        out_specs=[out_space] * len(out_shape) if many else out_space,
        scratch_shapes=list(scratch),
        compiler_params=pltpu.CompilerParams(vmem_limit_bytes=limit),
    )


def shape(dims, kind):
    return jax.ShapeDtypeStruct(dims, kind)


def plan_kernel(pieces_ref, lengths_ref, request_ref, where_ref):
    row = lax.broadcasted_iota(jnp.int32, (VOC, VOC), 0)
    col = lax.broadcasted_iota(jnp.int32, (VOC, VOC), 1)
    earlier = (row < col).astype(jnp.float32).astype(jnp.bfloat16)
    level = lax.broadcasted_iota(jnp.int32, (BLOCKS, VOC), 0)
    lengths = lengths_ref[...]
    base = jnp.zeros((BLOCKS, 1), jnp.float32)
    high_sum = jnp.zeros((BLOCKS, CAP), jnp.float32)
    low_sum = jnp.zeros((BLOCKS, CAP), jnp.float32)
    for k in range(PIECES):
        piece = pieces_ref[k : k + 1, :]
        live = lengths > k
        block = jnp.where(live, piece >> 11, BLOCKS)
        local = piece & (SHARD - 1)
        onehot = (block == level).astype(jnp.float32)
        onehot16 = onehot.astype(jnp.bfloat16)
        before = dot(onehot16, earlier) + base
        rank = jnp.sum(before * onehot, axis=0, keepdims=True).astype(jnp.int32)
        base = base + jnp.sum(onehot, axis=1, keepdims=True)
        at_rank = rank == level
        high = jnp.where(at_rank, (local >> 6).astype(jnp.float32), 0.0).astype(jnp.bfloat16)
        low = jnp.where(at_rank, (local & 63).astype(jnp.float32), 0.0).astype(jnp.bfloat16)
        high_sum = high_sum + dot_dims(onehot16, high, 1, 1)
        low_sum = low_sum + dot_dims(onehot16, low, 1, 1)
        where_ref[k : k + 1, :] = jnp.where(live, block * CAP + rank, -1)
    request_ref[...] = high_sum.astype(jnp.int32) * 64 + low_sum.astype(jnp.int32)


def fetch_kernel(wanted_ref, table_ref, out_ref, onehot_buf, table_buf, sem):
    width = FEAT // 2
    copies = []
    for h in range(2):
        columns = pl.ds(h * width, width)
        copies.append(
            pltpu.make_async_copy(table_ref.at[:, columns], table_buf.at[:, columns], sem.at[h])
        )
        copies[h].start()
    eye = lax.broadcasted_iota(jnp.int32, (CAP, CAP), 0) == lax.broadcasted_iota(
        jnp.int32, (CAP, CAP), 1
    )
    lane = lax.broadcasted_iota(jnp.int32, (CAP, SHARD), 1)
    for g in range(BLOCKS):
        row = wanted_ref[g].astype(jnp.float32)
        column = jnp.sum(jnp.where(eye, row, 0.0), axis=1, keepdims=True).astype(jnp.int32)
        onehot_buf[g * CAP : (g + 1) * CAP, :] = (
            (lane == column).astype(jnp.float32).astype(jnp.bfloat16)
        )
    for h in range(2):
        copies[h].wait()
        columns = slice(h * width, (h + 1) * width)
        out_ref[:, columns] = dot(onehot_buf[...], table_buf[:, columns]).astype(jnp.bfloat16)


def embed_kernel(position_ref, table_ref, out_ref, onehot_buf, table_buf, out_buf, sem, out_sem):
    tile, count = 512, BLOCKS * VOC
    load = pltpu.make_async_copy(table_ref, table_buf, sem)
    load.start()
    columns = jnp.concatenate(
        [position_ref[...], jnp.zeros((VOC - count // VOC, VOC), jnp.int32)], axis=0
    ).T
    lane = lax.broadcasted_iota(jnp.int32, (VOC, count), 1)
    stores = []
    for i in range(count // tile):
        for j in range(tile // VOC):
            n = i * (tile // VOC) + j
            onehot_buf[i % 2, j * VOC : (j + 1) * VOC, :] = (
                (lane == columns[:, n : n + 1]).astype(jnp.float32).astype(jnp.bfloat16)
            )
        if i == 0:
            load.wait()
        rows = pl.ds(i * tile, tile)
        out_buf[rows, :] = dot(onehot_buf[i % 2], table_buf[...]).astype(jnp.bfloat16)
        stores.append(
            pltpu.make_async_copy(out_buf.at[rows], out_ref.at[rows], out_sem.at[i])
        )
        stores[i].start()
    for store in stores:
        store.wait()


def spread_kernel(gain_ref, where_ref, out_ref):
    lane = lax.broadcasted_iota(jnp.int32, (VOC, BLOCKS * CAP), 1)
    columns = jnp.concatenate(
        [where_ref[...], jnp.zeros((VOC - PIECES, VOC), jnp.int32)], axis=0
    ).T
    total = jnp.zeros((VOC, BLOCKS * CAP), jnp.float32)
    for k in range(PIECES):
        total = jnp.where(columns[:, k : k + 1] == lane, gain_ref[k], total)
    for term in range(3):
        part = total.astype(jnp.bfloat16)
        out_ref[term] = part
        total = total - part.astype(jnp.float32)


def pool_kernel(spread_ref, rows_ref, gain_ref, out_ref):
    rows = rows_ref[...]
    pooled = dot(spread_ref[2], rows) + dot(spread_ref[1], rows) + dot(spread_ref[0], rows)
    out_ref[...] = (pooled * gain_ref[...]).astype(jnp.bfloat16)


def split_two(value, lane):
    high = value.astype(jnp.bfloat16)
    low = (value - high.astype(jnp.float32)).astype(jnp.bfloat16)
    return jnp.where(
        lane == 0, high.astype(jnp.float32), jnp.where(lane == 1, low.astype(jnp.float32), 0.0)
    ).astype(jnp.bfloat16)


def gather_rows(place_ref, refs, rows_buf):
    z = place_ref[0]
    for step, ref in zip((0, -1, 1, -2, 2, -3, 3), refs):
        at = lax.rem(z + (step + NZ), NZ)
        rows_buf[pl.ds(pl.multiple_of(at * VOC, VOC), VOC), :] = ref[...]
    at = lax.rem(z + 4, NZ)
    half = VOC // 2
    rows_buf[pl.ds(pl.multiple_of(at * VOC, half), half), :] = refs[7][...]
    rows_buf[pl.ds(pl.multiple_of(at * VOC + half, half), half), :] = refs[8][...]


def project_out_kernel(place_ref, order_ref, scale_ref, *refs):
    keep_ref, give_ref, rows_buf, result_buf, square_buf = refs[-5:]
    core = place_ref[1]
    gather_rows(place_ref, refs[:9], rows_buf)
    for q in range(NY):
        result_buf[order_ref[q]] = dot(rows_buf[...], refs[9][q])
    lane = lax.broadcasted_iota(jnp.int32, (VOC, EXTRA), 1)
    scale = scale_ref[...]
    for i in range(PARTS):
        wide = rows_buf[i * VOC : (i + 1) * VOC, :].astype(jnp.float32)
        square = jnp.sum(wide * wide * scale, axis=1, keepdims=True)
        square_buf[i] = split_two(square, lane)
    for i in range(NX):
        mine, other = 2 * i + core, 2 * i + 1 - core
        for q in range(NY):
            columns = slice(q * 256, (q + 1) * 256)
            keep_ref[i, :, columns] = result_buf[q, pl.ds(pl.multiple_of(mine * VOC, VOC), VOC), :]
            give_ref[i, :, columns] = result_buf[
                q, pl.ds(pl.multiple_of(other * VOC, VOC), VOC), :
            ].astype(jnp.bfloat16)
        keep_ref[i, :, WIDE:] = square_buf[mine].astype(jnp.float32)
        give_ref[i, :, WIDE:] = square_buf[other]


def project_in_kernel(place_ref, *refs):
    weight_ref, out_ref, rows_buf = refs[-3:]
    gather_rows(place_ref, refs[:9], rows_buf)
    for q in range(NY):
        out_ref[:, q * 256 : (q + 1) * 256] = dot(rows_buf[...], weight_ref[q])


def add_kernel(place_ref, keep_ref, got_ref, *out_refs):
    x = place_ref[3] >> 1
    lane = lax.broadcasted_iota(jnp.int32, (VOC, EXTRA), 1)
    for k, out_ref in zip(SHIFTS, out_refs):
        i = lax.rem(x + (k + NX), NX)
        total = keep_ref[i] + got_ref[i].astype(jnp.float32)
        out_ref[:, :WIDE] = total[:, :WIDE].astype(jnp.bfloat16)
        square = jnp.sum(total[:, WIDE:], axis=1, keepdims=True)
        out_ref[:, WIDE:] = split_two(square, lane)


def total_of(refs):
    total = refs[0][...].astype(jnp.float32)
    for ref in refs[1:]:
        total = total + ref[...].astype(jnp.float32)
    return total


def norm_kernel(*refs):
    first_ref, second_ref, inverse_ref = refs[NX:]
    total = total_of(refs[:NX])
    square = jnp.sum(total[:, WIDE:], axis=1, keepdims=True)
    inverse = lax.rsqrt(square / D + EPSILON)
    rows = total[:, :WIDE] * inverse
    first_ref[...] = rows[:, :HALF].T.astype(jnp.bfloat16)
    second_ref[...] = rows[:, HALF:].T.astype(jnp.bfloat16)
    inverse_ref[...] = inverse


def scale_kernel(place_ref, inverse_ref, total_ref, *out_refs):
    rows = (total_ref[...] * inverse_ref[...]).astype(jnp.bfloat16)
    for q in range(NY):
        for k, out_ref in zip(SHIFTS, out_refs):

            @pl.when(lax.rem(place_ref[2] + (k + NY), NY) == q)
            def _():
                out_ref[:VOC, :] = rows[:, q * 256 : q * 256 + VOC]
                out_ref[VOC:, :] = rows[:, q * 256 + VOC : (q + 1) * 256]


def shift_by(value, axis, step):
    count = {"y": NY, "z": NZ, "x": NX, "c": NC}[axis]
    return lax.ppermute(value, axis, [(i, (i + step) % count) for i in range(count)])


def z_ring(rows, first, beside):
    p1, m1 = shift_by(rows, "z", 1), shift_by(rows, "z", -1)
    p2, m2 = shift_by(p1, "z", 1), shift_by(m1, "z", -1)
    p2, m2, made = lax.optimization_barrier((p2, m2, beside(p1)))
    p3, m3 = shift_by(p2, "z", 1), shift_by(m2, "z", -1)
    p4, m4 = shift_by(p3[:first], "z", 1), shift_by(m3[first:], "z", -1)
    return [rows, p1, m1, p2, m2, p3, m3, p4, m4], made


def y_all(block):
    return [block] + [shift_by(block, "y", -step) for step in SHIFTS[1:]]


def deal(blocks, axis):
    return [blocks[0]] + [shift_by(b, axis, k) for b, k in zip(blocks[1:], SHIFTS[1:])]


def accumulate(shifts, routes, arrays, place_ref, hidden_ref, total_ref, bufs):
    hidden_buf, rows_buf, hidden_sem, rows_sem = bufs
    y, z = place_ref[2], place_ref[0]
    waits = [[] for _ in shifts]
    for slot, step in enumerate(shifts):
        at = lax.rem(z + (step + NZ), NZ)
        for q in range(NY):
            copy = pltpu.make_async_copy(
                hidden_ref.at[2 * q + at // 4, :, pl.ds(pl.multiple_of((at % 4) * 256, 256), 256)],
                hidden_buf.at[slot, :, pl.ds(q * 256, 256)],
                hidden_sem.at[slot, q],
            )
            copy.start()
            waits[slot].append(copy)
        for number, (index, from_row, rows, dy, dz, to_row) in enumerate(routes):
            if dz != step:
                continue
            at_y = lax.rem(y + (dy + NY), NY)
            copy = pltpu.make_async_copy(
                arrays[index].at[pl.ds(from_row, rows)],
                rows_buf.at[slot, pl.ds(to_row, rows), pl.ds(pl.multiple_of(at_y * VOC, VOC), VOC)],
                rows_sem.at[number],
            )
            copy.start()
            waits[slot].append(copy)
    tile = 256
    for slot in range(len(shifts)):
        for copy in waits[slot]:
            copy.wait()
        for i in range(TOK // tile):
            rows = pl.ds(i * tile, tile)
            product = dot(hidden_buf[slot, rows, :], rows_buf[slot])
            total_ref[rows, :] = total_ref[rows, :] + product


def near_kernel(shifts, routes, count, place_ref, hidden_ref, *refs):
    arrays, total_ref = refs[:count], refs[count]
    total_ref[...] = jnp.zeros_like(total_ref)
    accumulate(shifts, routes, arrays, place_ref, hidden_ref, total_ref, refs[count + 1 :])


def middle_kernel(shifts, routes, count, place_ref, total_in, hidden_ref, *refs):
    arrays, total_ref = refs[:count], refs[count]
    total_ref[...] = total_in[...]
    accumulate(shifts, routes, arrays, place_ref, hidden_ref, total_ref, refs[count + 1 :])


def far_kernel(shifts, routes, count, place_ref, target_ref, total_in, hidden_ref, *refs):
    arrays, out_ref, total_ref = refs[:count], refs[count], refs[count + 1]
    total_ref[...] = total_in[...]
    accumulate(shifts, routes, arrays, place_ref, hidden_ref, total_ref, refs[count + 2 :])
    part = place_ref[3]
    tile = 256
    column = lax.broadcasted_iota(jnp.int32, (tile, NY * VOC), 1)
    targets = jnp.concatenate(
        [target_ref[...], jnp.zeros((VOC - TOK // VOC, VOC), jnp.int32)], axis=0
    ).T
    token_of = (column // VOC) * (NZ * VOC) + part * VOC + column % VOC
    lane = lax.broadcasted_iota(jnp.int32, (tile, 128), 1)
    for i in range(TOK // tile):
        rows = pl.ds(i * tile, tile)
        total = total_ref[rows, :]
        best = jnp.max(total, axis=1, keepdims=True)
        spread = jnp.sum(jnp.exp(total - best), axis=1, keepdims=True)
        wanted = jnp.concatenate(
            [targets[:, j : j + 1] for j in range(i * tile // VOC, (i + 1) * tile // VOC)], axis=0
        )
        hit = jnp.sum(jnp.where(token_of == wanted, total, 0.0), axis=1, keepdims=True)
        packed = jnp.where(lane == 0, best, jnp.where(lane == 1, spread, hit))
        turned = packed.T
        for j in range(tile // 128):
            out_ref[i * (tile // 128) + j] = turned[:8, j * 128 : (j + 1) * 128]


def merge_kernel(parts_ref, out_ref):
    best = parts_ref[0, 0:1, :]
    for i in range(1, PARTS):
        best = jnp.maximum(best, parts_ref[i, 0:1, :])
    spread = jnp.zeros_like(best)
    hit = jnp.zeros_like(best)
    for i in range(PARTS):
        spread = spread + parts_ref[i, 1:2, :] * jnp.exp(parts_ref[i, 0:1, :] - best)
        hit = hit + parts_ref[i, 2:3, :]
    out_ref[...] = best + jnp.log(spread) - hit


def swap(value, axes):
    return lax.all_to_all(value, axes, split_axis=0, concat_axis=0, tiled=True)


def after(value, *others):
    return lax.optimization_barrier((value, *others))[0]


def on_device(
    old_table, pieces, lengths, pos_gain, hyp_gain, w_in, w_out, hidden, token_ids, targets
):
    y, z = lax.axis_index("y"), lax.axis_index("z")
    core = lax.axis_index("c")
    part = lax.axis_index(("x", "c"))
    place = jnp.stack([z, core, y, part]).astype(jnp.int32)
    gain_row = hyp_gain.reshape(1, FEAT)

    hidden_all = lax.all_gather(hidden, ("x", "c"), axis=0)

    requests, where = call(
        plan_kernel,
        [shape((BLOCKS, CAP), jnp.int32), shape((PIECES, VOC), jnp.int32)],
        [VMEM, VMEM],
    )(pieces.T, lengths.reshape(1, VOC))
    wanted = swap(requests.reshape(BLOCKS, 1, CAP), ("y", "z"))
    found = call(
        fetch_kernel,
        shape((BLOCKS * CAP, FEAT), jnp.bfloat16),
        [VMEM, ANY],
        [
            pltpu.VMEM((BLOCKS * CAP, SHARD), jnp.bfloat16),
            pltpu.VMEM((SHARD, FEAT), jnp.bfloat16),
            pltpu.SemaphoreType.DMA((2,)),
        ],
        MOST,
    )(wanted, old_table)
    fetched = swap(found.reshape(BLOCKS, CAP, FEAT), ("y", "z"))
    spread = call(
        spread_kernel, shape((3, VOC, BLOCKS * CAP), jnp.bfloat16), [SMEM, VMEM]
    )(pos_gain, where)
    w_in_all = lax.all_gather(after(w_in, found), "y", axis=0)
    w_out_all = y_all(after(w_out, found))
    fetched, *w_out_all = lax.optimization_barrier((fetched, *w_out_all))
    pooled = call(pool_kernel, shape((VOC, FEAT), jnp.bfloat16), [VMEM, VMEM, VMEM])(
        spread, fetched.reshape(BLOCKS * CAP, FEAT), gain_row
    )

    group, w_out_all = z_ring(
        pooled, VOC // 2, lambda there: jnp.stack(lax.optimization_barrier((w_out_all, there))[0])
    )
    inverse_gain = 1.0 / (gain_row * gain_row)

    order = (y + jnp.array(SHIFTS, jnp.int32)) % NY
    w_out_all, hidden_all = lax.optimization_barrier((w_out_all, hidden_all))
    wider = WIDE + EXTRA
    keep, give = call(
        project_out_kernel,
        [shape((NX, VOC, wider), jnp.float32), shape((NX, VOC, wider), jnp.bfloat16)],
        [SMEM, SMEM] + [VMEM] * 11,
        [
            pltpu.VMEM((NZ * VOC, FEAT), jnp.bfloat16),
            pltpu.VMEM((NY, NZ * VOC, 256), jnp.float32),
            pltpu.VMEM((PARTS, VOC, EXTRA), jnp.bfloat16),
        ],
    )(place, order, inverse_gain, *group, w_out_all)
    chip_out = call(
        add_kernel, [shape((VOC, wider), jnp.bfloat16)] * NX, [SMEM, VMEM, VMEM]
    )(place, keep, shift_by(give, "c", 1))

    def tie(*values):
        return lax.optimization_barrier(values)

    chip_out, w_in_all = tie(chip_out, w_in_all)
    partial_in = call(
        project_in_kernel,
        shape((NZ * VOC, WIDE), jnp.float32),
        [SMEM] + [VMEM] * 10,
        [pltpu.VMEM((NZ * VOC, FEAT), jnp.bfloat16)],
    )(place, *group, w_in_all)
    out_parts, partial_in = tie(deal(chip_out, "x"), partial_in)
    total_in = lax.psum_scatter(partial_in, ("x", "c"), scatter_dimension=0, tiled=True)
    first_half, second_half, inverse = call(
        norm_kernel,
        [shape((HALF, VOC), jnp.bfloat16)] * 2 + [shape((VOC, 1), jnp.float32)],
        [VMEM] * NX,
    )(*out_parts)

    def step(pair):
        return [shift_by(pair[0], "z", 1), shift_by(pair[1], "z", -1)]

    first_half, second_half = tie(first_half, second_half)
    own_y, a1 = tie(y_all(second_half), step([first_half, first_half]))
    column = jnp.concatenate(own_y, axis=0)
    pair_1 = [jnp.concatenate([a, column], axis=0) for a in a1]
    stack_1 = jnp.concatenate([first_half, *a1], axis=0)

    pair_1, stack_1 = tie(pair_1, stack_1)
    ring_1, pair_2 = tie(y_all(stack_1), step(pair_1))

    pair_2, stack_2 = tie(pair_2, jnp.concatenate([m[:HALF] for m in pair_2], axis=0))
    input_rows = call(
        scale_kernel, [shape((256, VOC), jnp.bfloat16)] * NY, [SMEM, VMEM, VMEM]
    )(place, inverse, total_in)
    ring_2, pair_3, input_rows = tie(y_all(stack_2), step(pair_2), input_rows)

    stack_3 = [m[:HALF] for m in pair_3]
    stacks = [jnp.concatenate([*stack_3, chunk], axis=0) for chunk in input_rows]
    pair_3, stacks = tie(pair_3, stacks)
    def take(kind, array, entries):
        for entry in entries:
            kind[1].append((len(kind[0]), *entry))
        kind[0].append(array)

    def column_at(low, dz):
        return [(low + i * HALF, HALF, dy, dz, HALF) for i, dy in enumerate(SHIFTS)]

    def others(shifts, arrays):
        return list(zip(shifts, arrays))[1:]

    def buffers(shifts, routes):
        return [
            pltpu.VMEM((len(shifts), TOK, WIDE), jnp.bfloat16),
            pltpu.VMEM((len(shifts), WIDE, NY * VOC), jnp.bfloat16),
            pltpu.SemaphoreType.DMA((len(shifts), NY)),
            pltpu.SemaphoreType.DMA((len(routes),)),
        ]

    near, middle, far = ([], []), ([], []), ([], [])
    take(near, column, column_at(0, 0))
    take(near, first_half, [(0, HALF, 0, 0, 0)])
    for a, dz in zip(a1, (-1, 1)):
        take(near, a, [(0, HALF, 0, dz, 0)])
    for m, dz in zip(pair_2, (-1, 1)):
        take(near, m, [(0, HALF, 0, 2 * dz, 0), *column_at(HALF, dz)])
    for m, dz in zip(pair_3, (-1, 1)):
        take(near, m, column_at(HALF, 2 * dz))
    for dy, array in others(SHIFTS, ring_1):
        take(near, array, [(i * HALF, HALF, dy, dz, 0) for i, dz in enumerate((0, -1, 1))])
    for dy, array in others(SHIFTS, ring_2):
        take(near, array, [(i * HALF, HALF, dy, dz, 0) for i, dz in enumerate((-2, 2))])

    logits_shape = shape((TOK, NY * VOC), jnp.float32)
    near_shifts, middle_shifts, far_shifts = (0, -1, 1, -2, 2), (-3, 3), (4,)
    total = call(
        lambda *refs: near_kernel(near_shifts, near[1], len(near[0]), *refs),
        logits_shape,
        [SMEM, ANY] + [ANY] * len(near[0]),
        buffers(near_shifts, near[1]),
        MOST,
    )(place, hidden_all, *near[0])
    ring_3, pair_4, total = tie(deal(stacks, "y"), step(pair_3), total)
    chunks = [array[2 * HALF :] for array in ring_3]
    chunks = [jnp.concatenate([c[:VOC], c[VOC:]], axis=1) for c in chunks]
    in_table = lax.all_gather(jnp.concatenate(chunks, axis=0), ("x", "c"), axis=0)

    for m, dz in zip(pair_3, (-1, 1)):
        take(middle, m, [(0, HALF, 0, 3 * dz, 0)])
    for m, dz in zip(pair_4, (-1, 1)):
        take(middle, m, column_at(HALF, 3 * dz))
    for dy, array in others([-k for k in SHIFTS], ring_3):
        take(middle, array, [(i * HALF, HALF, dy, dz, 0) for i, dz in enumerate((-3, 3))])
    last = [
        [pair_4[0][HALF : 3 * HALF], pair_3[0][:HALF], ring_3[1][:HALF]],
        [pair_4[1][3 * HALF :], ring_3[2][HALF : 2 * HALF], ring_3[3][HALF : 2 * HALF]],
    ]
    last, total = tie([jnp.concatenate(blocks, axis=0) for blocks in last], total)
    total = call(
        lambda *refs: middle_kernel(middle_shifts, middle[1], len(middle[0]), *refs),
        logits_shape,
        [SMEM, VMEM, ANY] + [ANY] * len(middle[0]),
        buffers(middle_shifts, middle[1]),
        MOST,
    )(place, total, hidden_all, *middle[0])
    last, total = tie(step(last), total)
    for half, array in enumerate(last):
        cut = slice(2 * half, 2 * half + 2)
        entries = [(i * HALF, HALF, dy, 4, HALF) for i, dy in enumerate(SHIFTS[cut])]
        dealt = [-k for k in SHIFTS[cut]]
        entries += [((2 + i) * HALF, HALF, dy, 4, 0) for i, dy in enumerate(dealt)]
        take(far, array, entries)

    back = (y - (token_ids >> 10)) & 3
    back = back ^ (back >> 1)
    position = ((token_ids >> 7) & 7) * (NY * VOC) + back * VOC + (token_ids & 127)
    embedded = call(
        embed_kernel,
        shape((BLOCKS * VOC, 256), jnp.bfloat16),
        [VMEM, ANY],
        [
            pltpu.VMEM((2, 512, BLOCKS * VOC), jnp.bfloat16),
            pltpu.VMEM((BLOCKS * VOC, 256), jnp.bfloat16),
            pltpu.VMEM((BLOCKS * VOC, 256), jnp.bfloat16),
            pltpu.SemaphoreType.DMA(()),
            pltpu.SemaphoreType.DMA((BLOCKS * VOC // 512,)),
        ],
        MOST,
        ANY,
    )(position.reshape(-1, VOC), in_table.reshape(BLOCKS * VOC, 256))

    stats = call(
        lambda *refs: far_kernel(far_shifts, far[1], len(far[0]), *refs),
        shape((PARTS, 8, 128), jnp.float32),
        [SMEM, VMEM, VMEM, ANY] + [ANY] * len(far[0]),
        [pltpu.VMEM((TOK, NY * VOC), jnp.float32), *buffers(far_shifts, far[1])],
        MOST,
    )(place, targets.reshape(-1, VOC), total, hidden_all, *far[0])
    merged, embedded = tie(swap(stats, ("x", "c")), embedded)
    loss = call(merge_kernel, shape((1, 128), jnp.float32), [VMEM])(merged)
    return (embedded, loss.reshape(128))


def solution(mesh):
    grid = Mesh(mesh.devices.reshape(NY, NZ, NX, NC), ("y", "z", "x", "c"))
    vocab, seq = ("y", "z"), ("x", "c")
    return jax.shard_map(
        on_device,
        mesh=grid,
        in_specs=(
            P(vocab, seq),
            P(vocab, None),
            P(vocab),
            P(),
            P(seq),
            P(seq, vocab),
            P(seq, vocab),
            P(vocab, seq),
            P(seq),
            P(vocab),
        ),
        out_specs=(P(seq, vocab), P((*vocab, *seq))),
        check_vma=False,
    )
```

```python
import jax
import jax.numpy as jnp
from jax import lax
from jax.experimental import pallas as pl
from jax.experimental.pallas import tpu as pltpu
from jax.sharding import Mesh
from jax.sharding import PartitionSpec as P

EPSILON = 1e-05
NY, NZ, NX, NC = 4, 8, 4, 2
BLOCKS = NY * NZ
PARTS = NX * NC
D = 8192
VOC = 128
PIECES = 8
SHARD = 2048
CAP = 32
FEAT = D // PARTS
WIDE = D // NZ
EXTRA = 128
TOK = 1024
HALF = WIDE // 2
MIB = 1 << 20
MOST = 56 * MIB
SHIFTS = (0, 1, -1, 2)

VMEM = pl.BlockSpec(memory_space=pltpu.VMEM)
SMEM = pl.BlockSpec(memory_space=pltpu.SMEM)
ANY = pl.BlockSpec(memory_space=pltpu.HBM)


def dot(left, right):
    return jnp.dot(left, right, preferred_element_type=jnp.float32)


def dot_dims(left, right, left_dim, right_dim):
    return lax.dot_general(
        left, right, (((left_dim,), (right_dim,)), ((), ())), preferred_element_type=jnp.float32
    )


def call(kernel, out_shape, in_specs, scratch=(), limit=16 * MIB, out_space=VMEM):
    many = isinstance(out_shape, (tuple, list))
    return pl.pallas_call(
        kernel,
        out_shape=out_shape,
        in_specs=in_specs,
        out_specs=[out_space] * len(out_shape) if many else out_space,
        scratch_shapes=list(scratch),
        compiler_params=pltpu.CompilerParams(vmem_limit_bytes=limit),
    )


def shape(dims, kind):
    return jax.ShapeDtypeStruct(dims, kind)


def plan_kernel(pieces_ref, lengths_ref, request_ref, where_ref):
    row = lax.broadcasted_iota(jnp.int32, (VOC, VOC), 0)
    col = lax.broadcasted_iota(jnp.int32, (VOC, VOC), 1)
    earlier = (row < col).astype(jnp.float32).astype(jnp.bfloat16)
    level = lax.broadcasted_iota(jnp.int32, (BLOCKS, VOC), 0)
    lengths = lengths_ref[...]
    base = jnp.zeros((BLOCKS, 1), jnp.float32)
    high_sum = jnp.zeros((BLOCKS, CAP), jnp.float32)
    low_sum = jnp.zeros((BLOCKS, CAP), jnp.float32)
    for k in range(PIECES):
        piece = pieces_ref[k : k + 1, :]
        live = lengths > k
        block = jnp.where(live, piece >> 11, BLOCKS)
        local = piece & (SHARD - 1)
        onehot = (block == level).astype(jnp.float32)
        onehot16 = onehot.astype(jnp.bfloat16)
        before = dot(onehot16, earlier) + base
        rank = jnp.sum(before * onehot, axis=0, keepdims=True).astype(jnp.int32)
        base = base + jnp.sum(onehot, axis=1, keepdims=True)
        at_rank = rank == level
        high = jnp.where(at_rank, (local >> 6).astype(jnp.float32), 0.0).astype(jnp.bfloat16)
        low = jnp.where(at_rank, (local & 63).astype(jnp.float32), 0.0).astype(jnp.bfloat16)
        high_sum = high_sum + dot_dims(onehot16, high, 1, 1)
        low_sum = low_sum + dot_dims(onehot16, low, 1, 1)
        where_ref[k : k + 1, :] = jnp.where(live, block * CAP + rank, -1)
    request_ref[...] = high_sum.astype(jnp.int32) * 64 + low_sum.astype(jnp.int32)


def fetch_kernel(wanted_ref, table_ref, out_ref, onehot_buf, table_buf, sem):
    width = FEAT // 2
    copies = []
    for h in range(2):
        columns = pl.ds(h * width, width)
        copies.append(
            pltpu.make_async_copy(table_ref.at[:, columns], table_buf.at[:, columns], sem.at[h])
        )
        copies[h].start()
    eye = lax.broadcasted_iota(jnp.int32, (CAP, CAP), 0) == lax.broadcasted_iota(
        jnp.int32, (CAP, CAP), 1
    )
    lane = lax.broadcasted_iota(jnp.int32, (CAP, SHARD), 1)
    for g in range(BLOCKS):
        row = wanted_ref[g].astype(jnp.float32)
        column = jnp.sum(jnp.where(eye, row, 0.0), axis=1, keepdims=True).astype(jnp.int32)
        onehot_buf[g * CAP : (g + 1) * CAP, :] = (
            (lane == column).astype(jnp.float32).astype(jnp.bfloat16)
        )
    for h in range(2):
        copies[h].wait()
        columns = slice(h * width, (h + 1) * width)
        out_ref[:, columns] = dot(onehot_buf[...], table_buf[:, columns]).astype(jnp.bfloat16)


def embed_kernel(position_ref, table_ref, out_ref, onehot_buf, table_buf, out_buf, sem, out_sem):
    tile, count = 512, BLOCKS * VOC
    load = pltpu.make_async_copy(table_ref, table_buf, sem)
    load.start()
    columns = jnp.concatenate(
        [position_ref[...], jnp.zeros((VOC - count // VOC, VOC), jnp.int32)], axis=0
    ).T
    lane = lax.broadcasted_iota(jnp.int32, (VOC, count), 1)
    stores = []
    for i in range(count // tile):
        for j in range(tile // VOC):
            n = i * (tile // VOC) + j
            onehot_buf[i % 2, j * VOC : (j + 1) * VOC, :] = (
                (lane == columns[:, n : n + 1]).astype(jnp.float32).astype(jnp.bfloat16)
            )
        if i == 0:
            load.wait()
        rows = pl.ds(i * tile, tile)
        out_buf[rows, :] = dot(onehot_buf[i % 2], table_buf[...]).astype(jnp.bfloat16)
        stores.append(
            pltpu.make_async_copy(out_buf.at[rows], out_ref.at[rows], out_sem.at[i])
        )
        stores[i].start()
    for store in stores:
        store.wait()


def spread_kernel(gain_ref, where_ref, out_ref):
    lane = lax.broadcasted_iota(jnp.int32, (VOC, BLOCKS * CAP), 1)
    columns = jnp.concatenate(
        [where_ref[...], jnp.zeros((VOC - PIECES, VOC), jnp.int32)], axis=0
    ).T
    total = jnp.zeros((VOC, BLOCKS * CAP), jnp.float32)
    for k in range(PIECES):
        total = jnp.where(columns[:, k : k + 1] == lane, gain_ref[k], total)
    for term in range(3):
        part = total.astype(jnp.bfloat16)
        out_ref[term] = part
        total = total - part.astype(jnp.float32)


def pool_kernel(spread_ref, rows_ref, gain_ref, out_ref):
    rows = rows_ref[...]
    pooled = dot(spread_ref[2], rows) + dot(spread_ref[1], rows) + dot(spread_ref[0], rows)
    out_ref[...] = (pooled * gain_ref[...]).astype(jnp.bfloat16)


def split_two(value, lane):
    high = value.astype(jnp.bfloat16)
    low = (value - high.astype(jnp.float32)).astype(jnp.bfloat16)
    return jnp.where(
        lane == 0, high.astype(jnp.float32), jnp.where(lane == 1, low.astype(jnp.float32), 0.0)
    ).astype(jnp.bfloat16)


def gather_rows(place_ref, refs, rows_buf):
    z = place_ref[0]
    for step, ref in zip((0, -1, 1, -2, 2, -3, 3, 4), refs):
        at = lax.rem(z + (step + NZ), NZ)
        rows_buf[pl.ds(pl.multiple_of(at * VOC, VOC), VOC), :] = ref[...]


def project_out_kernel(place_ref, order_ref, scale_ref, *refs):
    keep_ref, give_ref, rows_buf, result_buf, square_buf = refs[-5:]
    core = place_ref[1]
    gather_rows(place_ref, refs[:8], rows_buf)
    for q in range(NY):
        result_buf[order_ref[q]] = dot(rows_buf[...], refs[8][q])
    lane = lax.broadcasted_iota(jnp.int32, (VOC, EXTRA), 1)
    scale = scale_ref[...]
    for i in range(PARTS):
        wide = rows_buf[i * VOC : (i + 1) * VOC, :].astype(jnp.float32)
        square = jnp.sum(wide * wide * scale, axis=1, keepdims=True)
        square_buf[i] = split_two(square, lane)
    for i in range(NX):
        mine, other = 2 * i + core, 2 * i + 1 - core
        for q in range(NY):
            columns = slice(q * 256, (q + 1) * 256)
            keep_ref[i, :, columns] = result_buf[q, pl.ds(pl.multiple_of(mine * VOC, VOC), VOC), :]
            give_ref[i, :, columns] = result_buf[
                q, pl.ds(pl.multiple_of(other * VOC, VOC), VOC), :
            ].astype(jnp.bfloat16)
        keep_ref[i, :, WIDE:] = square_buf[mine].astype(jnp.float32)
        give_ref[i, :, WIDE:] = square_buf[other]


def project_in_kernel(place_ref, *refs):
    weight_ref, out_ref, rows_buf = refs[-3:]
    gather_rows(place_ref, refs[:8], rows_buf)
    for q in range(NY):
        out_ref[:, q * 256 : (q + 1) * 256] = dot(rows_buf[...], weight_ref[q])


def add_kernel(place_ref, keep_ref, got_ref, *out_refs):
    x = place_ref[3] >> 1
    lane = lax.broadcasted_iota(jnp.int32, (VOC, EXTRA), 1)
    for k, out_ref in zip(SHIFTS, out_refs):
        i = lax.rem(x + (k + NX), NX)
        total = keep_ref[i] + got_ref[i].astype(jnp.float32)
        out_ref[:, :WIDE] = total[:, :WIDE].astype(jnp.bfloat16)
        square = jnp.sum(total[:, WIDE:], axis=1, keepdims=True)
        out_ref[:, WIDE:] = split_two(square, lane)


def total_of(refs):
    total = refs[0][...].astype(jnp.float32)
    for ref in refs[1:]:
        total = total + ref[...].astype(jnp.float32)
    return total


def norm_kernel(*refs):
    first_ref, second_ref, inverse_ref = refs[NX:]
    total = total_of(refs[:NX])
    square = jnp.sum(total[:, WIDE:], axis=1, keepdims=True)
    inverse = lax.rsqrt(square / D + EPSILON)
    rows = total[:, :WIDE] * inverse
    first_ref[...] = rows[:, :HALF].T.astype(jnp.bfloat16)
    second_ref[...] = rows[:, HALF:].T.astype(jnp.bfloat16)
    inverse_ref[...] = inverse


def scale_kernel(place_ref, inverse_ref, total_ref, *out_refs):
    rows = (total_ref[...] * inverse_ref[...]).astype(jnp.bfloat16)
    for q in range(NY):
        for k, out_ref in zip(SHIFTS, out_refs):

            @pl.when(lax.rem(place_ref[2] + (k + NY), NY) == q)
            def _():
                out_ref[:VOC, :] = rows[:, q * 256 : q * 256 + VOC]
                out_ref[VOC:, :] = rows[:, q * 256 + VOC : (q + 1) * 256]


def shift_by(value, axis, step):
    count = {"y": NY, "z": NZ, "x": NX, "c": NC}[axis]
    return lax.ppermute(value, axis, [(i, (i + step) % count) for i in range(count)])


def z_ring(rows, beside):
    p1, m1 = shift_by(rows, "z", 1), shift_by(rows, "z", -1)
    p2, m2 = shift_by(p1, "z", 1), shift_by(m1, "z", -1)
    p2, m2, made = lax.optimization_barrier((p2, m2, beside(p1)))
    p3, m3 = shift_by(p2, "z", 1), shift_by(m2, "z", -1)
    p4 = shift_by(p3, "z", 1)
    return [rows, p1, m1, p2, m2, p3, m3, p4], made


def y_all(block):
    return [block] + [shift_by(block, "y", -step) for step in SHIFTS[1:]]


def deal(blocks, axis):
    return [blocks[0]] + [shift_by(b, axis, k) for b, k in zip(blocks[1:], SHIFTS[1:])]


def accumulate(shifts, routes, arrays, place_ref, hidden_ref, total_ref, bufs):
    hidden_buf, rows_buf, hidden_sem, rows_sem = bufs
    y, z = place_ref[2], place_ref[0]
    waits = [[] for _ in shifts]
    for slot, step in enumerate(shifts):
        at = lax.rem(z + (step + NZ), NZ)
        for q in range(NY):
            copy = pltpu.make_async_copy(
                hidden_ref.at[2 * q + at // 4, :, pl.ds(pl.multiple_of((at % 4) * 256, 256), 256)],
                hidden_buf.at[slot, :, pl.ds(q * 256, 256)],
                hidden_sem.at[slot, q],
            )
            copy.start()
            waits[slot].append(copy)
        for number, (index, from_row, rows, dy, dz, to_row) in enumerate(routes):
            if dz != step:
                continue
            at_y = lax.rem(y + (dy + NY), NY)
            copy = pltpu.make_async_copy(
                arrays[index].at[pl.ds(from_row, rows)],
                rows_buf.at[slot, pl.ds(to_row, rows), pl.ds(pl.multiple_of(at_y * VOC, VOC), VOC)],
                rows_sem.at[number],
            )
            copy.start()
            waits[slot].append(copy)
    tile = 256
    for slot in range(len(shifts)):
        for copy in waits[slot]:
            copy.wait()
        for i in range(TOK // tile):
            rows = pl.ds(i * tile, tile)
            product = dot(hidden_buf[slot, rows, :], rows_buf[slot])
            total_ref[rows, :] = total_ref[rows, :] + product


def near_kernel(shifts, routes, count, place_ref, hidden_ref, *refs):
    arrays, total_ref = refs[:count], refs[count]
    total_ref[...] = jnp.zeros_like(total_ref)
    accumulate(shifts, routes, arrays, place_ref, hidden_ref, total_ref, refs[count + 1 :])


def middle_kernel(shifts, routes, count, place_ref, total_in, hidden_ref, *refs):
    arrays, total_ref = refs[:count], refs[count]
    total_ref[...] = total_in[...]
    accumulate(shifts, routes, arrays, place_ref, hidden_ref, total_ref, refs[count + 1 :])


def far_kernel(shifts, routes, count, place_ref, target_ref, total_in, hidden_ref, *refs):
    arrays, out_ref, total_ref = refs[:count], refs[count], refs[count + 1]
    total_ref[...] = total_in[...]
    accumulate(shifts, routes, arrays, place_ref, hidden_ref, total_ref, refs[count + 2 :])
    part = place_ref[3]
    tile = 256
    column = lax.broadcasted_iota(jnp.int32, (tile, NY * VOC), 1)
    targets = jnp.concatenate(
        [target_ref[...], jnp.zeros((VOC - TOK // VOC, VOC), jnp.int32)], axis=0
    ).T
    token_of = (column // VOC) * (NZ * VOC) + part * VOC + column % VOC
    lane = lax.broadcasted_iota(jnp.int32, (tile, 128), 1)
    for i in range(TOK // tile):
        rows = pl.ds(i * tile, tile)
        total = total_ref[rows, :]
        best = jnp.max(total, axis=1, keepdims=True)
        spread = jnp.sum(jnp.exp(total - best), axis=1, keepdims=True)
        wanted = jnp.concatenate(
            [targets[:, j : j + 1] for j in range(i * tile // VOC, (i + 1) * tile // VOC)], axis=0
        )
        hit = jnp.sum(jnp.where(token_of == wanted, total, 0.0), axis=1, keepdims=True)
        packed = jnp.where(lane == 0, best, jnp.where(lane == 1, spread, hit))
        turned = packed.T
        for j in range(tile // 128):
            out_ref[i * (tile // 128) + j] = turned[:8, j * 128 : (j + 1) * 128]


def merge_kernel(parts_ref, out_ref):
    best = parts_ref[0, 0:1, :]
    for i in range(1, PARTS):
        best = jnp.maximum(best, parts_ref[i, 0:1, :])
    spread = jnp.zeros_like(best)
    hit = jnp.zeros_like(best)
    for i in range(PARTS):
        spread = spread + parts_ref[i, 1:2, :] * jnp.exp(parts_ref[i, 0:1, :] - best)
        hit = hit + parts_ref[i, 2:3, :]
    out_ref[...] = best + jnp.log(spread) - hit


def swap(value, axes):
    return lax.all_to_all(value, axes, split_axis=0, concat_axis=0, tiled=True)


def after(value, *others):
    return lax.optimization_barrier((value, *others))[0]


def on_device(
    old_table, pieces, lengths, pos_gain, hyp_gain, w_in, w_out, hidden, token_ids, targets
):
    y, z = lax.axis_index("y"), lax.axis_index("z")
    core = lax.axis_index("c")
    part = lax.axis_index(("x", "c"))
    place = jnp.stack([z, core, y, part]).astype(jnp.int32)
    gain_row = hyp_gain.reshape(1, FEAT)

    hidden_all = lax.all_gather(hidden, ("x", "c"), axis=0)

    requests, where = call(
        plan_kernel,
        [shape((BLOCKS, CAP), jnp.int32), shape((PIECES, VOC), jnp.int32)],
        [VMEM, VMEM],
    )(pieces.T, lengths.reshape(1, VOC))
    wanted = swap(requests.reshape(BLOCKS, 1, CAP), ("y", "z"))
    found = call(
        fetch_kernel,
        shape((BLOCKS * CAP, FEAT), jnp.bfloat16),
        [VMEM, ANY],
        [
            pltpu.VMEM((BLOCKS * CAP, SHARD), jnp.bfloat16),
            pltpu.VMEM((SHARD, FEAT), jnp.bfloat16),
            pltpu.SemaphoreType.DMA((2,)),
        ],
        MOST,
    )(wanted, old_table)
    fetched = swap(found.reshape(BLOCKS, CAP, FEAT), ("y", "z"))
    spread = call(
        spread_kernel, shape((3, VOC, BLOCKS * CAP), jnp.bfloat16), [SMEM, VMEM]
    )(pos_gain, where)
    w_in_all = lax.all_gather(after(w_in, found), "y", axis=0)
    w_out_all = y_all(after(w_out, found))
    fetched, *w_out_all = lax.optimization_barrier((fetched, *w_out_all))
    pooled = call(pool_kernel, shape((VOC, FEAT), jnp.bfloat16), [VMEM, VMEM, VMEM])(
        spread, fetched.reshape(BLOCKS * CAP, FEAT), gain_row
    )

    group, w_out_all = z_ring(
        pooled, lambda there: jnp.stack(lax.optimization_barrier((w_out_all, there))[0])
    )
    inverse_gain = 1.0 / (gain_row * gain_row)

    order = (y + jnp.array(SHIFTS, jnp.int32)) % NY
    w_out_all, hidden_all = lax.optimization_barrier((w_out_all, hidden_all))
    wider = WIDE + EXTRA
    keep, give = call(
        project_out_kernel,
        [shape((NX, VOC, wider), jnp.float32), shape((NX, VOC, wider), jnp.bfloat16)],
        [SMEM, SMEM] + [VMEM] * 10,
        [
            pltpu.VMEM((NZ * VOC, FEAT), jnp.bfloat16),
            pltpu.VMEM((NY, NZ * VOC, 256), jnp.float32),
            pltpu.VMEM((PARTS, VOC, EXTRA), jnp.bfloat16),
        ],
    )(place, order, inverse_gain, *group, w_out_all)
    chip_out = call(
        add_kernel, [shape((VOC, wider), jnp.bfloat16)] * NX, [SMEM, VMEM, VMEM]
    )(place, keep, shift_by(give, "c", 1))

    def tie(*values):
        return lax.optimization_barrier(values)

    chip_out, w_in_all = tie(chip_out, w_in_all)
    partial_in = call(
        project_in_kernel,
        shape((NZ * VOC, WIDE), jnp.float32),
        [SMEM] + [VMEM] * 9,
        [pltpu.VMEM((NZ * VOC, FEAT), jnp.bfloat16)],
    )(place, *group, w_in_all)
    out_parts, partial_in = tie(deal(chip_out, "x"), partial_in)
    total_in = lax.psum_scatter(partial_in, ("x", "c"), scatter_dimension=0, tiled=True)
    first_half, second_half, inverse = call(
        norm_kernel,
        [shape((HALF, VOC), jnp.bfloat16)] * 2 + [shape((VOC, 1), jnp.float32)],
        [VMEM] * NX,
    )(*out_parts)

    def step(pair):
        return [shift_by(pair[0], "z", 1), shift_by(pair[1], "z", -1)]

    first_half, second_half = tie(first_half, second_half)
    own_y, a1 = tie(y_all(second_half), step([first_half, first_half]))
    column = jnp.concatenate(own_y, axis=0)
    pair_1 = [jnp.concatenate([a, column], axis=0) for a in a1]
    stack_1 = jnp.concatenate([first_half, *a1], axis=0)

    pair_1, stack_1 = tie(pair_1, stack_1)
    ring_1, pair_2 = tie(y_all(stack_1), step(pair_1))

    pair_2, stack_2 = tie(pair_2, jnp.concatenate([m[:HALF] for m in pair_2], axis=0))
    input_rows = call(
        scale_kernel, [shape((256, VOC), jnp.bfloat16)] * NY, [SMEM, VMEM, VMEM]
    )(place, inverse, total_in)
    ring_2, pair_3, input_rows = tie(y_all(stack_2), step(pair_2), input_rows)

    stack_3 = [m[:HALF] for m in pair_3]
    stacks = [jnp.concatenate([*stack_3, chunk], axis=0) for chunk in input_rows]
    pair_3, stacks = tie(pair_3, stacks)
    def take(kind, array, entries):
        for entry in entries:
            kind[1].append((len(kind[0]), *entry))
        kind[0].append(array)

    def column_at(low, dz):
        return [(low + i * HALF, HALF, dy, dz, HALF) for i, dy in enumerate(SHIFTS)]

    def others(shifts, arrays):
        return list(zip(shifts, arrays))[1:]

    def buffers(shifts, routes):
        return [
            pltpu.VMEM((len(shifts), TOK, WIDE), jnp.bfloat16),
            pltpu.VMEM((len(shifts), WIDE, NY * VOC), jnp.bfloat16),
            pltpu.SemaphoreType.DMA((len(shifts), NY)),
            pltpu.SemaphoreType.DMA((len(routes),)),
        ]

    near, middle, far = ([], []), ([], []), ([], [])
    take(near, column, column_at(0, 0))
    take(near, first_half, [(0, HALF, 0, 0, 0)])
    for a, dz in zip(a1, (-1, 1)):
        take(near, a, [(0, HALF, 0, dz, 0)])
    for m, dz in zip(pair_2, (-1, 1)):
        take(near, m, [(0, HALF, 0, 2 * dz, 0), *column_at(HALF, dz)])
    for m, dz in zip(pair_3, (-1, 1)):
        take(near, m, column_at(HALF, 2 * dz))
    for dy, array in others(SHIFTS, ring_1):
        take(near, array, [(i * HALF, HALF, dy, dz, 0) for i, dz in enumerate((0, -1, 1))])
    for dy, array in others(SHIFTS, ring_2):
        take(near, array, [(i * HALF, HALF, dy, dz, 0) for i, dz in enumerate((-2, 2))])

    logits_shape = shape((TOK, NY * VOC), jnp.float32)
    near_shifts, middle_shifts, far_shifts = (0, -1, 1, -2, 2), (-3, 3), (4,)
    total = call(
        lambda *refs: near_kernel(near_shifts, near[1], len(near[0]), *refs),
        logits_shape,
        [SMEM, ANY] + [ANY] * len(near[0]),
        buffers(near_shifts, near[1]),
        MOST,
    )(place, hidden_all, *near[0])
    ring_3, pair_4, total = tie(deal(stacks, "y"), step(pair_3), total)
    chunks = [array[2 * HALF :] for array in ring_3]
    chunks = [jnp.concatenate([c[:VOC], c[VOC:]], axis=1) for c in chunks]
    in_table = lax.all_gather(jnp.concatenate(chunks, axis=0), ("x", "c"), axis=0)

    for m, dz in zip(pair_3, (-1, 1)):
        take(middle, m, [(0, HALF, 0, 3 * dz, 0)])
    for m, dz in zip(pair_4, (-1, 1)):
        take(middle, m, column_at(HALF, 3 * dz))
    for dy, array in others([-k for k in SHIFTS], ring_3):
        take(middle, array, [(i * HALF, HALF, dy, dz, 0) for i, dz in enumerate((-3, 3))])
    last = [
        [pair_4[0][HALF : 3 * HALF], pair_3[0][:HALF], ring_3[1][:HALF]],
        [pair_4[1][3 * HALF :], ring_3[2][HALF : 2 * HALF], ring_3[3][HALF : 2 * HALF]],
    ]
    last, total = tie([jnp.concatenate(blocks, axis=0) for blocks in last], total)
    total = call(
        lambda *refs: middle_kernel(middle_shifts, middle[1], len(middle[0]), *refs),
        logits_shape,
        [SMEM, VMEM, ANY] + [ANY] * len(middle[0]),
        buffers(middle_shifts, middle[1]),
        MOST,
    )(place, total, hidden_all, *middle[0])
    last, total = tie(step(last), total)
    for half, array in enumerate(last):
        cut = slice(2 * half, 2 * half + 2)
        entries = [(i * HALF, HALF, dy, 4, HALF) for i, dy in enumerate(SHIFTS[cut])]
        dealt = [-k for k in SHIFTS[cut]]
        entries += [((2 + i) * HALF, HALF, dy, 4, 0) for i, dy in enumerate(dealt)]
        take(far, array, entries)

    back = (y - (token_ids >> 10)) & 3
    back = back ^ (back >> 1)
    position = ((token_ids >> 7) & 7) * (NY * VOC) + back * VOC + (token_ids & 127)
    embedded = call(
        embed_kernel,
        shape((BLOCKS * VOC, 256), jnp.bfloat16),
        [VMEM, ANY],
        [
            pltpu.VMEM((2, 512, BLOCKS * VOC), jnp.bfloat16),
            pltpu.VMEM((BLOCKS * VOC, 256), jnp.bfloat16),
            pltpu.VMEM((BLOCKS * VOC, 256), jnp.bfloat16),
            pltpu.SemaphoreType.DMA(()),
            pltpu.SemaphoreType.DMA((BLOCKS * VOC // 512,)),
        ],
        MOST,
        ANY,
    )(position.reshape(-1, VOC), in_table.reshape(BLOCKS * VOC, 256))

    stats = call(
        lambda *refs: far_kernel(far_shifts, far[1], len(far[0]), *refs),
        shape((PARTS, 8, 128), jnp.float32),
        [SMEM, VMEM, VMEM, ANY] + [ANY] * len(far[0]),
        [pltpu.VMEM((TOK, NY * VOC), jnp.float32), *buffers(far_shifts, far[1])],
        MOST,
    )(place, targets.reshape(-1, VOC), total, hidden_all, *far[0])
    merged, embedded = tie(swap(stats, ("x", "c")), embedded)
    loss = call(merge_kernel, shape((1, 128), jnp.float32), [VMEM])(merged)
    return (embedded, loss.reshape(128))


def solution(mesh):
    grid = Mesh(mesh.devices.reshape(NY, NZ, NX, NC), ("y", "z", "x", "c"))
    vocab, seq = ("y", "z"), ("x", "c")
    return jax.shard_map(
        on_device,
        mesh=grid,
        in_specs=(
            P(vocab, seq),
            P(vocab, None),
            P(vocab),
            P(),
            P(seq),
            P(seq, vocab),
            P(seq, vocab),
            P(vocab, seq),
            P(seq),
            P(vocab),
        ),
        out_specs=(P(seq, vocab), P((*vocab, *seq))),
        check_vma=False,
    )
```
